128 devices in a mesh: enc: 16 (over y, x_lo, core), dec: 8 (over x_hi, z).
Axes of the slice: x: 4 (x_hi: 2, x_lo: 2; x = x_hi * 2 + x_lo), y: 4, z: 4, core: 2. Of those that a mesh axis runs over, the one named last changes fastest.
Arguments:
- tokens: bfloat16 [2048, 4096], P('dec'), may hold values from -21 to 21
- w_query: bfloat16 [4096, 4096], P(None, 'enc'), may hold values from -0.09375 to 0.09375
- context: bfloat16 [4096, 1024], P('enc'), may hold values from -6 to 6
- w_key: bfloat16 [1024, 4096], P(None, 'enc'), may hold values from -0.1875 to 0.1875
- w_value: bfloat16 [1024, 4096], P(None, 'enc'), may hold values from -0.1875 to 0.1875
- self_query: bfloat16 [2048, 4096], P('dec', 'enc'), may hold values from -90 to 90
- self_key: bfloat16 [2048, 4096], P('dec', 'enc'), may hold values from -4 to 4
- self_value: bfloat16 [2048, 4096], P('dec', 'enc'), may hold values from -6 to 6
- grad_self: bfloat16 [2048, 4096], P('dec', 'enc'), may hold values from -6 to 6
- grad_cross: bfloat16 [2048, 4096], P('dec', 'enc'), may hold values from -6 to 6
Outputs:
- self_out: bfloat16 [2048, 4096], P('dec', 'enc')
- grad_self_query: float32 [2048, 4096], P('dec', 'enc')
- grad_self_key: float32 [2048, 4096], P('dec', 'enc')
- grad_self_value: float32 [2048, 4096], P('dec', 'enc')
- cross_out: bfloat16 [2048, 4096], P('dec', 'enc')
- grad_w_query: float32 [4096, 4096], P('dec', 'enc')
- grad_w_key: float32 [1024, 4096], P('dec', 'enc')
- grad_w_value: float32 [1024, 4096], P('dec', 'enc')
The draws below stay inside these ranges and needn't reach their ends.
All inputs are finite; a program needn't handle non-finite values.
Results may differ from the reference program's by a relative error of at most 0.029.
The reference program's roundings to bfloat16 on the way count: a program that leaves them out, or rounds other values in their place, can miss the bound.
Values may be sent and summed in bfloat16 or wider, within the bound.
A program may use at most 128 MiB of HBM per device.

```python
import jax
import jax.numpy as jnp
from jax import lax

D = 4096
HD = 128
D_ENC = 1024
TOK_DEV = 256
HEADS = 32
DEC_TOKENS = 2048
CTX = 4096
N_DEC = 8


def shared_keys(key):
    return jnp.clip(jax.random.normal(key, (DEC_TOKENS, HEADS * HD), jnp.float32), -4.0, 4.0)


def draw_self_key(key, part):
    return shared_keys(key).astype(jnp.bfloat16)


def draw_self_query(key, part):
    key = jax.random.fold_in(key, 5)
    own_values = jnp.clip(jax.random.normal(key, (DEC_TOKENS, HEADS * HD), jnp.float32), -4.0, 4.0)
    return own_values.astype(jnp.bfloat16)


def draw_tokens(key, part):
    key = jax.random.fold_in(key, 7)
    return jnp.clip(jax.random.normal(key, (DEC_TOKENS, D), jnp.float32), -6.0, 6.0).astype(jnp.bfloat16)


def shard_levels(rng, extent, cuts, low, top_value):
    def one(dim, shards_of):
        steps = jax.random.uniform(jax.random.fold_in(jax.random.fold_in(rng, 6), dim), (shards_of,), jnp.float32, low / len(cuts), top_value / len(cuts))
        return jnp.repeat(jnp.exp(steps), extent[dim] // shards_of).reshape((-1,) + (1,) * (len(extent) - dim - 1))

    level = one(*cuts[0])
    for cut in cuts[1:]:
        level = level * one(*cut)
    return level


def scatter_about(rng, extent, deviation, limit, shards=(), held_as=jnp.bfloat16):
    entries = deviation * jax.random.normal(rng, extent, jnp.float32)
    if shards:
        entries = entries * shard_levels(rng, extent, shards, -0.22, 0.18)
    return jnp.clip(entries, -limit, limit).astype(held_as)


def setup_inputs(seed: int = 0) -> dict:
    arg_keys = jax.random.split(jax.random.key(seed), 11)
    tokens = draw_tokens(jax.random.fold_in(arg_keys[10], 71), 0)
    w_query = scatter_about(arg_keys[1], (D, HEADS * HD), D ** -0.5, 0.09375, ((1, 16),))
    context = scatter_about(arg_keys[2], (CTX, D_ENC), 1.0, 6.0, ((0, 16),))
    w_key = scatter_about(arg_keys[3], (D_ENC, HEADS * HD), D_ENC ** -0.5, 0.1875, ((1, 16),))
    w_value = scatter_about(arg_keys[4], (D_ENC, HEADS * HD), D_ENC ** -0.5, 0.1875, ((1, 16),))
    self_query = draw_self_query(jax.random.fold_in(arg_keys[10], 71), 0)
    self_key = draw_self_key(jax.random.fold_in(arg_keys[10], 71), 0)
    self_value = scatter_about(arg_keys[7], (DEC_TOKENS, HEADS * HD), 1.0, 6.0, ((0, 8), (1, 16)))
    grad_self = scatter_about(arg_keys[8], (DEC_TOKENS, HEADS * HD), 1.0, 6.0, ((0, 8), (1, 16)))
    grad_cross = scatter_about(arg_keys[9], (DEC_TOKENS, HEADS * HD), 1.0, 6.0, ((0, 8), (1, 16)))
    return {"tokens": tokens, "w_query": w_query, "context": context, "w_key": w_key, "w_value": w_value, "self_query": self_query, "self_key": self_key, "self_value": self_value, "grad_self": grad_self, "grad_cross": grad_cross}


def head_terms(head_query, head_key, head_value, head_grad, visible, blocked):
    score_scale = HD ** -0.5
    scores = jnp.dot(head_query, head_key.T, preferred_element_type=jnp.float32) * score_scale
    scores = jnp.where(visible, scores, -1e30)
    row_max = jnp.max(scores, axis=1, keepdims=True)
    weights = jnp.exp(scores - row_max)
    normaliser = jnp.sum(weights, axis=1, keepdims=True)
    head_context = (jnp.dot(weights.astype(jnp.bfloat16), head_value, preferred_element_type=jnp.float32) / normaliser).astype(jnp.bfloat16)
    log_norm = row_max + jnp.log(normaliser)
    probability = jnp.exp(scores - log_norm)
    grad_prob = jnp.dot(head_grad, head_value.T, preferred_element_type=jnp.float32)
    row_delta = jnp.sum(head_grad.astype(jnp.float32) * head_context.astype(jnp.float32), axis=1, keepdims=True)
    grad_score = (probability * (grad_prob - row_delta) * score_scale).astype(jnp.bfloat16)
    grad_query = jnp.dot(grad_score, head_key, preferred_element_type=jnp.float32)
    prob_low = probability.astype(jnp.bfloat16)
    if blocked:
        score_blocks = lax.optimization_barrier(grad_score).astype(jnp.float32).reshape(N_DEC, TOK_DEV, -1)
        prob_blocks = lax.optimization_barrier(prob_low).astype(jnp.float32).reshape(N_DEC, TOK_DEV, -1)
        query_blocks = head_query.astype(jnp.float32).reshape(N_DEC, TOK_DEV, HD)
        grad_blocks = head_grad.astype(jnp.float32).reshape(N_DEC, TOK_DEV, HD)
        key_parts = jnp.einsum("bnc,bnd->bcd", score_blocks, query_blocks)
        value_parts = jnp.einsum("bnc,bnd->bcd", prob_blocks, grad_blocks)
        key_parts = lax.optimization_barrier(key_parts.astype(jnp.bfloat16)).astype(jnp.float32)
        value_parts = lax.optimization_barrier(value_parts.astype(jnp.bfloat16)).astype(jnp.float32)
        grad_key = jnp.sum(key_parts, axis=0)
        grad_value = jnp.sum(value_parts, axis=0)
    else:
        grad_key = jnp.dot(grad_score.T, head_query, preferred_element_type=jnp.float32)
        grad_value = jnp.dot(prob_low.T, head_grad, preferred_element_type=jnp.float32)
    return head_context, grad_query, grad_key, grad_value


def to_heads(array):
    return array.reshape(array.shape[0], HEADS, HD).transpose(1, 0, 2)


def from_heads(array):
    return array.transpose(1, 0, 2).reshape(array.shape[1], HEADS * HD)


def reference(tokens, w_query, context, w_key, w_value, self_query, self_key, self_value, grad_self, grad_cross):
    cross_q = jnp.dot(tokens, w_query, preferred_element_type=jnp.float32).astype(jnp.bfloat16)
    cross_k = jnp.dot(context, w_key, preferred_element_type=jnp.float32).astype(jnp.bfloat16)
    cross_v = jnp.dot(context, w_value, preferred_element_type=jnp.float32).astype(jnp.bfloat16)
    position = jnp.arange(DEC_TOKENS)
    visible = position[:, None] >= position[None, :]

    def self_head(inputs):
        return head_terms(inputs[0], inputs[1], inputs[2], inputs[3], visible, False)

    def cross_head(inputs):
        return head_terms(inputs[0], inputs[1], inputs[2], inputs[3], True, True)

    self_terms = lax.map(self_head, (to_heads(self_query), to_heads(self_key), to_heads(self_value), to_heads(grad_self)))
    cross_terms = lax.map(cross_head, (to_heads(cross_q), to_heads(cross_k), to_heads(cross_v), to_heads(grad_cross)))
    self_out, grad_sq, grad_sk, grad_sv = [from_heads(item) for item in self_terms]
    cross_out, cross_dq, cross_dk, cross_dv = [from_heads(item) for item in cross_terms]
    grad_w_query = jnp.dot(tokens.T, cross_dq.astype(jnp.bfloat16), preferred_element_type=jnp.float32)
    wide_context = context.astype(jnp.float32).T
    grad_w_key = jnp.dot(wide_context, cross_dk, precision=lax.Precision.HIGHEST)
    grad_w_value = jnp.dot(wide_context, cross_dv, precision=lax.Precision.HIGHEST)
    return (self_out, grad_sq, grad_sk, grad_sv, cross_out, grad_w_query, grad_w_key, grad_w_value)
```

```python
import jax
import jax.numpy as jnp
from jax import lax
from jax.experimental import pallas as pl
from jax.experimental.pallas import tpu as pltpu
from jax.sharding import PartitionSpec as P

MESH = pl.DeviceIdType.MESH
HD = 128
SCALE = HD ** -0.5
ROWS = 256
F32 = jnp.float32
BF16 = jnp.bfloat16


def nn(a, b):
    return jnp.dot(a, b, preferred_element_type=F32)


def nt(a, b):
    return lax.dot_general(a, b, (((1,), (1,)), ((), ())), preferred_element_type=F32)


def kernel(
    tok_h, wq_h, ctx_h, wk_h, wv_h, sq_h, sk_h, sv_h, gs_h, gc_h,
    o_self, o_dsq, o_dsk, o_dsv, o_cross, o_gwq, o_gwk, o_gwv,
    tok, wq, wkv, wkvt, own, gc, ctx, kvt, wst, dpst, mst, dkvt,
    cm, cl, cacc, sm, sl, sacc, blk, stat, tb, dqt, wsend, wrecv,
    lsem, ssem, ctx_sem, sib_sem, blk_sem, stat_sem, tok_sem, tokg_sem, tsib_sem, dq_sem, w_sem,
):
    e = lax.axis_index("enc")
    d = lax.axis_index("dec")
    y, low = e // 4, e % 4
    core = e % 2
    yup = lax.rem(y + 1, 4) * 4 + low
    ydn = lax.rem(y + 3, 4) * 4 + low
    yfar = lax.rem(y + 2, 4) * 4 + low
    sib = e + 1 - 2 * core
    xflip = e + 2 - 4 * ((e // 2) % 2)
    xh = d // 4

    def peer(m):
        out = d
        for bit in (1, 2, 4):
            if m & bit:
                out = out + bit - 2 * bit * ((d // bit) % 2)
        return out

    dev = {
        "yup": (yup, d), "ydn": (ydn, d), "yfar": (yfar, d), "sib": (sib, d),
        "xi": (xflip, d), "xo": (xflip, peer(4)),
    }
    partner = [(e, peer(m)) for m in range(8)]

    barrier = pltpu.get_barrier_semaphore()
    greet = list(dev.values()) + partner[1:]
    for target in greet:
        pl.semaphore_signal(barrier, inc=1, device_id=target, device_id_type=MESH)

    loads = []

    def load(src, dst):
        copy = pltpu.make_async_copy(src, dst, lsem.at[len(loads)])
        copy.start()
        loads.append(copy)
        return copy

    l_own = [load(r, own.at[i]) for i, r in enumerate((sk_h, sv_h, sq_h, gs_h))]
    l_ctx = load(ctx_h, ctx.at[0, 0])
    l_wk = load(wk_h, wkv.at[:, pl.ds(0, ROWS)])
    l_wv = load(wv_h, wkv.at[:, pl.ds(ROWS, ROWS)])
    l_gc = load(gc_h, gc)
    l_tok = load(tok_h, tok)
    l_wq = load(wq_h, wq)

    sends = []

    def send(src, dst, rsem, target):
        copy = pltpu.make_async_remote_copy(
            src_ref=src, dst_ref=dst, send_sem=ssem.at[len(sends)], recv_sem=rsem,
            device_id=target, device_id_type=MESH,
        )
        copy.start()
        sends.append(copy)

    def arrived(dst, rsem):
        pltpu.make_async_remote_copy(
            src_ref=dst, dst_ref=dst, send_sem=ssem.at[0], recv_sem=rsem,
            device_id=dev["sib"], device_id_type=MESH,
        ).wait_recv()

    half = ROWS // 2

    def part(k, h, side=0):
        return ctx.at[k, side, pl.ds(h * half, half), :]

    def whole_out(k, h, src, target):
        send(src, part(k, h), ctx_sem.at[k, h], target)

    def got(k, h):
        arrived(part(k, h), ctx_sem.at[k, h])

    def share(k, h):
        send(part(k, h), part(k, h, 1), sib_sem.at[k, h], dev["sib"])

    def shared(k):
        for h in range(2):
            arrived(part(k, h, 1), sib_sem.at[k, h])

    for c in l_own:
        c.wait()
    l_ctx.wait()
    pl.semaphore_wait(barrier, len(greet))

    whole_out(6, 0, part(0, 0), dev["yup"])
    whole_out(2, 1, part(0, 1), dev["ydn"])
    whole_out(1, 0, part(0, 0), dev["xi"])
    whole_out(1, 1, part(0, 1), dev["xo"])
    share(0, 0)
    share(0, 1)
    whole_out(6, 1, part(0, 1), dev["yup"])
    whole_out(2, 0, part(0, 0), dev["ydn"])

    def own_block(m):
        first = 2 * (1 - ((d // (1 if m == 1 else 2 if m < 4 else 4)) % 2))
        return own.at[pl.ds(2 - first, 2)]

    def blk_out(m, slot, src):
        send(src, blk.at[slot], blk_sem.at[slot], partner[m])

    blk_out(4, 4, own_block(4))
    blk_out(1, 1, own_block(1))
    blk_out(3, 3, own_block(3))
    blk_out(2, 2, own_block(2))

    l_wk.wait()
    l_wv.wait()
    wkvt[...] = wkv[...].T
    l_tok.wait()
    l_wq.wait()
    cq32 = nn(tok[...], wq[...])
    cq = cq32.astype(BF16)
    cqt = cq.T
    l_gc.wait()
    gcv = gc[...]
    gct = gcv.T

    def hs(h):
        return slice(h * HD, (h + 1) * HD)

    def cross_forward(k, first):
        x = ctx[k].reshape(2 * ROWS, ctx.shape[3])
        kv = nt(wkvt[...], x).astype(BF16)
        cols = slice(k * 2 * ROWS, (k + 1) * 2 * ROWS)
        kvt[:, cols] = kv
        for h in range(2):
            s = nn(cq[:, hs(h)], kv[hs(h)]) * SCALE
            top = jnp.max(s, axis=1, keepdims=True)
            if not first:
                old = cm[h]
                top = jnp.maximum(old, top)
            w = jnp.exp(s - top)
            wst[h, :, cols] = w
            dpst[h, :, cols] = nn(gcv[:, hs(h)], kv[hs(2 + h)])
            add_l = jnp.sum(w, axis=1, keepdims=True)
            add_o = nt(w.astype(BF16), kv[hs(2 + h)])
            if not first:
                fix = jnp.exp(old - top)
                add_l = add_l + cl[h] * fix
                add_o = add_o + cacc[h] * fix
            cm[h] = top
            cl[h] = add_l
            cacc[h] = add_o
            mst[k, h] = top

    shared(0)
    cross_forward(0, True)

    got(6, 0)
    whole_out(4, 0, part(6, 0), dev["yup"])
    whole_out(7, 0, part(6, 0), dev["xi"])
    share(6, 0)
    got(2, 1)
    whole_out(4, 1, part(2, 1), dev["ydn"])
    whole_out(3, 1, part(2, 1), dev["xo"])
    share(2, 1)
    for h in range(2):
        got(1, h)
        share(1, h)
    got(6, 1)
    whole_out(7, 1, part(6, 1), dev["xo"])
    share(6, 1)
    got(2, 0)
    whole_out(3, 0, part(2, 0), dev["xi"])
    share(2, 0)
    arrived(blk.at[4], blk_sem.at[4])
    for m in (1, 3, 2):
        blk_out(m, 4 + m, blk.at[4])
    lane = (y * 2 + core) * 32
    trows = pl.ds(pl.multiple_of(lane, 32), 32)

    def tcols(p):
        return pl.ds(pl.multiple_of(p * 512, 512), 512)

    for m in range(1, 8):
        send(tok.at[trows, tcols(partner[m][1])], tb.at[m, trows], tok_sem.at[m], partner[m])
    l_tb = load(tok.at[:, tcols(d)], tb.at[0])

    shared(1)
    cross_forward(1, False)
    shared(6)
    cross_forward(6, False)
    shared(2)
    cross_forward(2, False)

    got(7, 0)
    whole_out(5, 0, part(7, 0), dev["yup"])
    share(7, 0)
    got(3, 1)
    whole_out(5, 1, part(3, 1), dev["ydn"])
    share(3, 1)
    got(4, 0)
    share(4, 0)
    got(4, 1)
    share(4, 1)
    got(7, 1)
    share(7, 1)
    got(3, 0)
    share(3, 0)
    shared(4)
    cross_forward(4, False)
    shared(7)
    cross_forward(7, False)
    shared(3)
    cross_forward(3, False)
    for m in range(1, 8):
        arrived(tb.at[m, trows], tok_sem.at[m])
    l_tb.wait()

    def trange(ee):
        return pl.ds(pl.multiple_of((ee // 4 * 2 + ee % 2) * 32, 32), 32)

    moved = tb.at[pl.ds(1, 7), trows]
    for i, name in enumerate(("yup", "ydn", "yfar", "sib")):
        send(moved, moved, tokg_sem.at[i], dev[name])
    got(5, 0)
    share(5, 0)
    got(5, 1)
    share(5, 1)
    shared(5)
    cross_forward(5, False)

    for h in range(2):
        norm = cl[h]
        out = (cacc[h] / norm).astype(BF16)
        o_cross[:, hs(h)] = out
        g = gcv[:, hs(h)]
        lse = cm[h] + jnp.log(norm)
        delta = jnp.sum(g.astype(F32) * out.astype(F32), axis=1, keepdims=True)
        qt = cqt[hs(h)]
        gt = gct[hs(h)]
        dq = None
        for k in range(8):
            cols = slice(k * 2 * ROWS, (k + 1) * 2 * ROWS)
            p = wst[h, :, cols] * jnp.exp(mst[k, h] - lse)
            ds = (p * (dpst[h, :, cols] - delta) * SCALE).astype(BF16)
            add = nt(ds, kvt[hs(h), cols])
            dq = add if dq is None else dq + add
            dkvt[hs(h), cols] = nn(qt, ds).astype(BF16)
            dkvt[hs(2 + h), cols] = nn(gt, p.astype(BF16)).astype(BF16)
        dqt[0, hs(h), :] = dq.astype(BF16).T
    for m in (4, 5, 6, 7, 2, 1, 3):
        send(dqt.at[0], dqt.at[m], dq_sem.at[m], partner[m])

    odd = d % 2
    ctx2 = ctx.reshape(16 * ROWS, ctx.shape[3])
    for j in (2, 3, 1, 0):
        lo = partner[2 * j][1] // 2 * 256
        piece = nn(dkvt[...], ctx2[:, pl.ds(pl.multiple_of(lo, 256), 256)]).astype(BF16)
        for b in range(2):
            wsend[j, b] = piece[:, b * 128:(b + 1) * 128]
        for r in range(2):
            m = 2 * j + r
            if m:
                src = wsend.at[j, odd if r == 0 else 1 - odd]
                send(src, wrecv.at[m], w_sem.at[m], partner[m])

    row = lax.broadcasted_iota(jnp.int32, (ROWS, ROWS), 0)
    col = lax.broadcasted_iota(jnp.int32, (ROWS, ROWS), 1)

    def xor_slot(p):
        a, b = d, p
        out = 0
        for bit in (1, 2, 4):
            out = out + bit * (((a // bit) + (b // bit)) % 2)
        return out

    for h in range(2):
        s = jnp.where(row >= col, nt(own[2, :, hs(h)], own[0, :, hs(h)]) * SCALE, -1e30)
        top = jnp.max(s, axis=1, keepdims=True)
        w = jnp.exp(s - top)
        sm[h] = top
        sl[h] = jnp.sum(w, axis=1, keepdims=True)
        sacc[h] = nn(w.astype(BF16), own[1, :, hs(h)])

    for m in (1, 2, 3, 5, 6, 7):
        arrived(blk.at[m], blk_sem.at[m])

    def self_forward(p, carry):
        slot = xor_slot(p)
        for h in range(2):
            s = nt(own[2, :, hs(h)], blk[slot, 0, :, hs(h)]) * SCALE
            old = sm[h]
            top = jnp.maximum(old, jnp.max(s, axis=1, keepdims=True))
            w = jnp.exp(s - top)
            fix = jnp.exp(old - top)
            sm[h] = top
            sl[h] = sl[h] * fix + jnp.sum(w, axis=1, keepdims=True)
            sacc[h] = sacc[h] * fix + nn(w.astype(BF16), blk[slot, 1, :, hs(h)])
        return carry

    lax.fori_loop(0, d, self_forward, 0)
    for h in range(2):
        norm = sl[h]
        out = (sacc[h] / norm).astype(BF16)
        o_self[:, hs(h)] = out
        g = own[3, :, hs(h)]
        lse = sm[h] + jnp.log(norm)
        delta = jnp.sum(g.astype(F32) * out.astype(F32), axis=1, keepdims=True)
        sm[h] = lse
        sl[h] = delta
        stat[0, 2 * h:2 * h + 1, :] = jnp.broadcast_to(lse, (ROWS, HD)).T[0:1]
        stat[0, 2 * h + 1:2 * h + 2, :] = jnp.broadcast_to(delta, (ROWS, HD)).T[0:1]
    for m in range(1, 8):
        send(stat.at[0], stat.at[m], stat_sem.at[m], partner[m])

    def query_grad(h, s, v, k):
        p = jnp.exp(s - sm[h])
        dp = nt(own[3, :, hs(h)], v)
        return nn((p * (dp - sl[h]) * SCALE).astype(BF16), k)

    for h in range(2):
        k = own[0, :, hs(h)]
        s = jnp.where(row >= col, nt(own[2, :, hs(h)], k) * SCALE, -1e30)
        o_dsq[:, hs(h)] = query_grad(h, s, own[1, :, hs(h)], k)

    def self_query(p, carry):
        slot = xor_slot(p)
        for h in range(2):
            k = blk[slot, 0, :, hs(h)]
            s = nt(own[2, :, hs(h)], k) * SCALE
            o_dsq[:, hs(h)] += query_grad(h, s, blk[slot, 1, :, hs(h)], k)
        return carry

    lax.fori_loop(0, d, self_query, 0)

    def key_grad(h, st, q, g, lse, delta):
        p = jnp.exp(st - lse)
        dp = nt(own[1, :, hs(h)], g)
        ds = (p * (dp - delta) * SCALE).astype(BF16)
        return nn(ds, q), nn(p.astype(BF16), g)

    for h in range(2):
        q, g = own[2, :, hs(h)], own[3, :, hs(h)]
        st = jnp.where(col >= row, nt(own[0, :, hs(h)], q) * SCALE, -1e30)
        dk, dv = key_grad(h, st, q, g, stat[0, 2 * h:2 * h + 1], stat[0, 2 * h + 1:2 * h + 2])
        o_dsk[:, hs(h)] = dk
        o_dsv[:, hs(h)] = dv
    for m in range(1, 8):
        arrived(stat.at[m], stat_sem.at[m])

    def self_key(p, carry):
        slot = xor_slot(p)
        for h in range(2):
            q, g = blk[slot, 0, :, hs(h)], blk[slot, 1, :, hs(h)]
            st = nt(own[0, :, hs(h)], q) * SCALE
            dk, dv = key_grad(
                h, st, q, g, stat[slot, 2 * h:2 * h + 1], stat[slot, 2 * h + 1:2 * h + 2]
            )
            o_dsk[:, hs(h)] += dk
            o_dsv[:, hs(h)] += dv
        return carry

    lax.fori_loop(d + 1, 8, self_key, 0)

    for i, ee in enumerate((ydn, yup, yfar, sib)):
        spot = tb.at[pl.ds(1, 7), trange(ee)]
        arrived(spot, tokg_sem.at[i])
    others = []
    for i, ee in enumerate((ydn, yup, yfar)):
        spot = tb.at[pl.ds(1, 7), trange(ee)]
        send(spot, spot, tsib_sem.at[i], dev["sib"])
    for i, ee in enumerate((ydn, yup, yfar)):
        ss = ee + 1 - 2 * core
        arrived(tb.at[pl.ds(1, 7), trange(ss)], tsib_sem.at[i])
    gw = None
    for m in range(8):
        if m:
            arrived(dqt.at[m], dq_sem.at[m])
        add = nn(dqt[m], tb[m])
        gw = add if gw is None else gw + add
    o_gwq[...] = gw.T

    total = wsend[0, odd].astype(F32)
    for m in range(1, 8):
        arrived(wrecv.at[m], w_sem.at[m])
        total = total + wrecv[m].astype(F32)
    o_gwk[...] = total[0:256].T
    o_gwv[...] = total[256:512].T

    for copy in sends:
        copy.wait_send()


def body(*args):
    vm, any_ = pl.BlockSpec(memory_space=pltpu.VMEM), pl.BlockSpec(memory_space=pl.ANY)
    shape = jax.ShapeDtypeStruct
    block = (ROWS, ROWS)
    dma = pltpu.SemaphoreType.DMA
    return tuple(pl.pallas_call(
        kernel,
        out_shape=(
            shape(block, BF16), shape(block, F32), shape(block, F32), shape(block, F32),
            shape(block, BF16), shape((512, ROWS), F32), shape((128, ROWS), F32),
            shape((128, ROWS), F32),
        ),
        in_specs=[any_] * 10,
        out_specs=[vm] * 8,
        scratch_shapes=[
            pltpu.VMEM((256, 4096), BF16),
            pltpu.VMEM((4096, 256), BF16),
            pltpu.VMEM((1024, 512), BF16),
            pltpu.VMEM((512, 1024), BF16),
            pltpu.VMEM((4, 256, 256), BF16),
            pltpu.VMEM((256, 256), BF16),
            pltpu.VMEM((8, 2, 256, 1024), BF16),
            pltpu.VMEM((512, 4096), BF16),
            pltpu.VMEM((2, 256, 4096), F32),
            pltpu.VMEM((2, 256, 4096), F32),
            pltpu.VMEM((8, 2, 256, 1), F32),
            pltpu.VMEM((512, 4096), BF16),
            pltpu.VMEM((2, 256, 1), F32),
            pltpu.VMEM((2, 256, 1), F32),
            pltpu.VMEM((2, 256, 128), F32),
            pltpu.VMEM((2, 256, 1), F32),
            pltpu.VMEM((2, 256, 1), F32),
            pltpu.VMEM((2, 256, 128), F32),
            pltpu.VMEM((8, 2, 256, 256), BF16),
            pltpu.VMEM((8, 8, 256), F32),
            pltpu.VMEM((8, 256, 512), BF16),
            pltpu.VMEM((8, 256, 256), BF16),
            pltpu.VMEM((4, 2, 512, 128), BF16),
            pltpu.VMEM((8, 512, 128), BF16),
            dma((16,)), dma((80,)), dma((8, 2)), dma((8, 2)), dma((8,)), dma((8,)), dma((8,)),
            dma((4,)), dma((3,)), dma((8,)), dma((8,)),
        ],
        compiler_params=pltpu.CompilerParams(
            collective_id=0, has_side_effects=True, vmem_limit_bytes=62 << 20
        ),
        name="layer",
    )(*args))


def solution(mesh):
    placed = (
        P("dec", None), P(None, "enc"), P("enc", None), P(None, "enc"), P(None, "enc"),
    ) + (P("dec", "enc"),) * 5
    return jax.shard_map(
        body, mesh=mesh, in_specs=placed, out_specs=(P("dec", "enc"),) * 8, check_vma=False
    )
```

```python
import jax
import jax.numpy as jnp
from jax import lax
from jax.experimental import pallas as pl
from jax.experimental.pallas import tpu as pltpu
from jax.sharding import PartitionSpec as P

MESH = pl.DeviceIdType.MESH
HD = 128
SCALE = HD ** -0.5
ROWS = 256
F32 = jnp.float32
BF16 = jnp.bfloat16


def nn(a, b):
    return jnp.dot(a, b, preferred_element_type=F32)


def nt(a, b):
    return lax.dot_general(a, b, (((1,), (1,)), ((), ())), preferred_element_type=F32)


def kernel(
    tok_h, wq_h, ctx_h, wk_h, wv_h, sq_h, sk_h, sv_h, gs_h, gc_h,
    o_self, o_dsq, o_dsk, o_dsv, o_cross, o_gwq, o_gwk, o_gwv,
    tok, wq, wkv, wkvt, own, gc, ctx, kvt, wst, dpst, mst, dkvt,
    cm, cl, cacc, sst, sm, sl, sacc, blk, stat, tb, dqt, wown, wmine, wpeer, wz,
    lsem, ssem, ctx_sem, sib_sem, blk_sem, stat_sem, tok_sem, tokg_sem, tsib_sem, dq_sem, wp_sem,
    wz_sem,
):
    e = lax.axis_index("enc")
    d = lax.axis_index("dec")
    y, low = e // 4, e % 4
    core = e % 2
    yup = lax.rem(y + 1, 4) * 4 + low
    ydn = lax.rem(y + 3, 4) * 4 + low
    yfar = lax.rem(y + 2, 4) * 4 + low
    sib = e + 1 - 2 * core
    xflip = e + 2 - 4 * ((e // 2) % 2)
    xh = d // 4

    def peer(m):
        out = d
        for bit in (1, 2, 4):
            if m & bit:
                out = out + bit - 2 * bit * ((d // bit) % 2)
        return out

    dev = {
        "yup": (yup, d), "ydn": (ydn, d), "yfar": (yfar, d), "sib": (sib, d),
        "xi": (xflip, d), "xo": (xflip, peer(4)),
    }
    partner = [(e, peer(m)) for m in range(8)]

    barrier = pltpu.get_barrier_semaphore()
    greet = list(dev.values()) + partner[1:]
    for target in greet:
        pl.semaphore_signal(barrier, inc=1, device_id=target, device_id_type=MESH)

    loads = []

    def load(src, dst):
        copy = pltpu.make_async_copy(src, dst, lsem.at[len(loads)])
        copy.start()
        loads.append(copy)
        return copy

    l_own = [load(r, own.at[i]) for i, r in enumerate((sk_h, sv_h, sq_h, gs_h))]
    l_ctx = load(ctx_h, ctx.at[0, 0])
    l_wk = load(wk_h, wkv.at[:, pl.ds(0, ROWS)])
    l_wv = load(wv_h, wkv.at[:, pl.ds(ROWS, ROWS)])
    l_gc = load(gc_h, gc)
    l_tok = load(tok_h, tok)
    l_wq = load(wq_h, wq)

    sends = []

    def send(src, dst, rsem, target):
        copy = pltpu.make_async_remote_copy(
            src_ref=src, dst_ref=dst, send_sem=ssem.at[len(sends)], recv_sem=rsem,
            device_id=target, device_id_type=MESH,
        )
        copy.start()
        sends.append(copy)

    def arrived(dst, rsem):
        pltpu.make_async_remote_copy(
            src_ref=dst, dst_ref=dst, send_sem=ssem.at[0], recv_sem=rsem,
            device_id=dev["sib"], device_id_type=MESH,
        ).wait_recv()

    quarter = ROWS // 4

    def part(k, i, side=0):
        return ctx.at[k, side, pl.ds(i * quarter, quarter), :]

    def pass_on(src, k, i, target):
        send(src, part(k, i), ctx_sem.at[k, i], target)

    def got(k, i):
        arrived(part(k, i), ctx_sem.at[k, i])

    def share(k, i):
        send(part(k, i), part(k, i, 1), sib_sem.at[k, i], dev["sib"])

    def shared(k):
        for i in range(4):
            arrived(part(k, i, 1), sib_sem.at[k, i])

    for c in l_own:
        c.wait()
    l_ctx.wait()
    pl.semaphore_wait(barrier, len(greet))

    def own_block(m):
        bit = (d // (1 if m == 1 else 2 if m < 4 else 4)) % 2
        return own.at[pl.ds(2 * bit, 2)]

    def blk_out(m, slot, src):
        send(src, blk.at[slot], blk_sem.at[slot], partner[m])

    blk_out(4, 4, own_block(4))
    for i in (0, 1):
        pass_on(part(0, i), 6, i, dev["yup"])
        pass_on(part(0, 2 + i), 2, 2 + i, dev["ydn"])
        pass_on(part(0, i), 1, i, dev["xi"])
        pass_on(part(0, 2 + i), 1, 2 + i, dev["xo"])
    for i in range(4):
        share(0, i)
    for i in (0, 1):
        pass_on(part(0, 2 + i), 6, 2 + i, dev["yup"])
        pass_on(part(0, i), 2, i, dev["ydn"])
    blk_out(1, 1, own_block(1))
    blk_out(3, 3, own_block(3))
    blk_out(2, 2, own_block(2))

    l_wk.wait()
    l_wv.wait()
    wkvt[...] = wkv[...].T
    l_tok.wait()
    l_wq.wait()
    cq = nn(tok[...], wq[...]).astype(BF16)
    cqt = cq.T
    l_gc.wait()
    gcv = gc[...]
    gct = gcv.T

    def hs(h):
        return slice(h * HD, (h + 1) * HD)

    def cross_forward(k, first):
        x = ctx[k].reshape(2 * ROWS, ctx.shape[3])
        kv = nt(wkvt[...], x).astype(BF16)
        cols = slice(k * 2 * ROWS, (k + 1) * 2 * ROWS)
        kvt[:, cols] = kv
        for h in range(2):
            s = nn(cq[:, hs(h)], kv[hs(h)]) * SCALE
            top = jnp.max(s, axis=1, keepdims=True)
            if not first:
                old = cm[h]
                top = jnp.maximum(old, top)
            w = jnp.exp(s - top)
            wst[h, :, cols] = w
            dpst[h, :, cols] = nn(gcv[:, hs(h)], kv[hs(2 + h)])
            add_l = jnp.sum(w, axis=1, keepdims=True)
            add_o = nt(w.astype(BF16), kv[hs(2 + h)])
            if not first:
                fix = jnp.exp(old - top)
                add_l = add_l + cl[h] * fix
                add_o = add_o + cacc[h] * fix
            cm[h] = top
            cl[h] = add_l
            cacc[h] = add_o
            mst[k, h] = top

    row = lax.broadcasted_iota(jnp.int32, (ROWS, ROWS), 0)
    col = lax.broadcasted_iota(jnp.int32, (ROWS, ROWS), 1)

    def xor_slot(p):
        out = 0
        for bit in (1, 2, 4):
            out = out + bit * (((d // bit) + (p // bit)) % 2)
        return out

    def halves(f, x):
        return f(x[:, :HD], x[:, HD:])

    def self_scores(p, carry):
        slot = xor_slot(p)
        for h in range(2):
            s = nt(own[2, :, hs(h)], blk[slot, 0, :, hs(h)]) * SCALE
            sst[slot, h] = s
            sm[h] = jnp.maximum(sm[h], halves(jnp.maximum, s))
        return carry

    shared(0)
    cross_forward(0, True)
    for i in (0, 1):
        got(6, i)
        pass_on(part(6, i), 4, i, dev["yup"])
        pass_on(part(6, i), 7, i, dev["xi"])
        share(6, i)
        got(2, 2 + i)
        pass_on(part(2, 2 + i), 4, 2 + i, dev["ydn"])
        pass_on(part(2, 2 + i), 3, 2 + i, dev["xo"])
        share(2, 2 + i)
    for i in range(4):
        got(1, i)
        share(1, i)
    for h in range(2):
        s = jnp.where(row >= col, nt(own[2, :, hs(h)], own[0, :, hs(h)]) * SCALE, -1e30)
        sst[0, h] = s
        sm[h] = halves(jnp.maximum, s)
    arrived(blk.at[4], blk_sem.at[4])
    for m in (1, 3, 2):
        blk_out(m, 4 + m, blk.at[4])
    shared(1)
    cross_forward(1, False)
    for i in (0, 1):
        got(6, 2 + i)
        pass_on(part(6, 2 + i), 7, 2 + i, dev["xo"])
        share(6, 2 + i)
        got(2, i)
        pass_on(part(2, i), 3, i, dev["xi"])
        share(2, i)
    lane = (y * 2 + core) * 32
    trows = pl.ds(pl.multiple_of(lane, 32), 32)

    def tcols(p):
        return pl.ds(pl.multiple_of(p * 512, 512), 512)

    for m in range(1, 8):
        send(tok.at[trows, tcols(partner[m][1])], tb.at[m, trows], tok_sem.at[m], partner[m])
    l_tb = load(tok.at[:, tcols(d)], tb.at[0])
    shared(6)
    cross_forward(6, False)
    for i in (0, 1):
        got(7, i)
        pass_on(part(7, i), 5, i, dev["yup"])
        share(7, i)
        got(3, 2 + i)
        pass_on(part(3, 2 + i), 5, 2 + i, dev["ydn"])
        share(3, 2 + i)
    shared(2)
    cross_forward(2, False)
    for m in (1, 2, 3):
        arrived(blk.at[m], blk_sem.at[m])
    lax.fori_loop(4 * xh, d, self_scores, 0)
    for i in range(4):
        got(4, i)
        share(4, i)
    shared(4)
    cross_forward(4, False)
    for i in (0, 1):
        got(7, 2 + i)
        share(7, 2 + i)
        got(3, i)
        share(3, i)
    shared(7)
    cross_forward(7, False)
    shared(3)
    cross_forward(3, False)
    for m in range(1, 8):
        arrived(tb.at[m, trows], tok_sem.at[m])
    l_tb.wait()

    def trange(ee):
        return pl.ds(pl.multiple_of((ee // 4 * 2 + ee % 2) * 32, 32), 32)

    moved = tb.at[pl.ds(1, 7), trows]
    for i, name in enumerate(("yup", "ydn", "yfar", "sib")):
        send(moved, moved, tokg_sem.at[i], dev[name])
    for i in range(4):
        got(5, i)
        share(5, i)
    for m in (5, 6, 7):
        arrived(blk.at[m], blk_sem.at[m])
    lax.fori_loop(0, 4 * xh, self_scores, 0)
    tops = [jnp.max(sm[h], axis=1, keepdims=True) for h in range(2)]
    for h in range(2):
        w = jnp.exp(sst[0, h] - tops[h])
        sl[h] = halves(jnp.add, w)
        sacc[h] = nn(w.astype(BF16), own[1, :, hs(h)])
        sm[h] = jnp.broadcast_to(tops[h], (ROWS, HD))

    def self_weights(p, carry):
        slot = xor_slot(p)
        for h in range(2):
            w = jnp.exp(sst[slot, h] - sm[h, :, 0:1])
            sl[h] += halves(jnp.add, w)
            sacc[h] += nn(w.astype(BF16), blk[slot, 1, :, hs(h)])
        return carry

    lax.fori_loop(0, d, self_weights, 0)
    for h in range(2):
        norm = jnp.sum(sl[h], axis=1, keepdims=True)
        out = (sacc[h] / norm).astype(BF16)
        o_self[:, hs(h)] = out
        g = own[3, :, hs(h)]
        lse = tops[h] + jnp.log(norm)
        delta = jnp.sum(g.astype(F32) * out.astype(F32), axis=1, keepdims=True)
        sm[h] = jnp.broadcast_to(lse, (ROWS, HD))
        sl[h] = jnp.broadcast_to(delta, (ROWS, HD))
        stat[0, 2 * h:2 * h + 1, :] = sm[h].T[0:1]
        stat[0, 2 * h + 1:2 * h + 2, :] = sl[h].T[0:1]
    for m in range(1, 8):
        send(stat.at[0], stat.at[m], stat_sem.at[m], partner[m])
    shared(5)
    cross_forward(5, False)

    def weight_part(h, group):
        cols = pl.ds(pl.multiple_of(group * 512, 512), 512)
        return nn(dkvt[h], ctx.reshape(16 * ROWS, ctx.shape[3])[:, cols])

    def dq_slot(m, h):
        return dqt.at[m, pl.ds(h * HD, HD), :]

    for h in range(2):
        norm = cl[h]
        out = (cacc[h] / norm).astype(BF16)
        o_cross[:, hs(h)] = out
        g = gcv[:, hs(h)]
        lse = cm[h] + jnp.log(norm)
        delta = jnp.sum(g.astype(F32) * out.astype(F32), axis=1, keepdims=True)
        qt = cqt[hs(h)]
        gt = gct[hs(h)]
        dq = None
        for k in range(8):
            cols = slice(k * 2 * ROWS, (k + 1) * 2 * ROWS)
            p = wst[h, :, cols] * jnp.exp(mst[k, h] - lse)
            ds = (p * (dpst[h, :, cols] - delta) * SCALE).astype(BF16)
            add = nt(ds, kvt[hs(h), cols])
            dq = add if dq is None else dq + add
            dkvt[h, 0:HD, cols] = nn(qt, ds).astype(BF16)
            dkvt[h, HD:, cols] = nn(gt, p.astype(BF16)).astype(BF16)
        dqt[0, hs(h), :] = dq.astype(BF16).T
        for m in (4, 1, 3, 2):
            send(dq_slot(0, h), dq_slot(m, h), dq_sem.at[m, h], partner[m])
        piece = weight_part(h, 1 - xh).astype(BF16)
        for z in range(4):
            wmine[h, z] = piece[:, z * HD:(z + 1) * HD]
        send(wmine.at[h], wpeer.at[h], wp_sem.at[h], partner[4])

    def forward_dq(h):
        arrived(dq_slot(4, h), dq_sem.at[4, h])
        for m in (1, 3, 2):
            send(dq_slot(4, h), dq_slot(4 + m, h), dq_sem.at[4 + m, h], partner[m])

    forward_dq(0)
    for h in range(2):
        piece = weight_part(h, xh)
        for z in range(4):
            wown[h, z] = piece[:, z * HD:(z + 1) * HD]
    for i, ee in enumerate((ydn, yup, yfar, sib)):
        arrived(tb.at[pl.ds(1, 7), trange(ee)], tokg_sem.at[i])
    for i, ee in enumerate((ydn, yup, yfar)):
        spot = tb.at[pl.ds(1, 7), trange(ee)]
        send(spot, spot, tsib_sem.at[i], dev["sib"])
    forward_dq(1)

    def sum_and_pass(h):
        arrived(wpeer.at[h], wp_sem.at[h])
        wown[h] = wown[h] + wpeer[h].astype(F32)
        wpeer[h] = wown[h].astype(BF16)
        for m in (1, 3, 2):
            send(
                wpeer.at[h, partner[m][1] - 4 * xh], wz.at[m, h], wz_sem.at[m, h], partner[m]
            )

    sum_and_pass(0)

    def query_grad(h, s, v, k):
        p = jnp.exp(s - sm[h, :, 0:1])
        dp = nt(own[3, :, hs(h)], v)
        return nn((p * (dp - sl[h, :, 0:1]) * SCALE).astype(BF16), k)

    for h in range(2):
        o_dsq[:, hs(h)] = query_grad(h, sst[0, h], own[1, :, hs(h)], own[0, :, hs(h)])

    def self_query(p, carry):
        slot = xor_slot(p)
        for h in range(2):
            o_dsq[:, hs(h)] += query_grad(
                h, sst[slot, h], blk[slot, 1, :, hs(h)], blk[slot, 0, :, hs(h)]
            )
        return carry

    lax.fori_loop(0, d, self_query, 0)

    def key_grad(h, st, q, g, lse, delta):
        p = jnp.exp(st - lse)
        dp = nt(own[1, :, hs(h)], g)
        ds = (p * (dp - delta) * SCALE).astype(BF16)
        return nn(ds, q), nn(p.astype(BF16), g)

    for h in range(2):
        q, g = own[2, :, hs(h)], own[3, :, hs(h)]
        st = jnp.where(col >= row, nt(own[0, :, hs(h)], q) * SCALE, -1e30)
        dk, dv = key_grad(h, st, q, g, stat[0, 2 * h:2 * h + 1], stat[0, 2 * h + 1:2 * h + 2])
        o_dsk[:, hs(h)] = dk
        o_dsv[:, hs(h)] = dv
    for m in range(1, 8):
        arrived(stat.at[m], stat_sem.at[m])

    def self_key(p, carry):
        slot = xor_slot(p)
        for h in range(2):
            q, g = blk[slot, 0, :, hs(h)], blk[slot, 1, :, hs(h)]
            st = nt(own[0, :, hs(h)], q) * SCALE
            dk, dv = key_grad(
                h, st, q, g, stat[slot, 2 * h:2 * h + 1], stat[slot, 2 * h + 1:2 * h + 2]
            )
            o_dsk[:, hs(h)] += dk
            o_dsv[:, hs(h)] += dv
        return carry

    lax.fori_loop(d + 1, 8, self_key, 0)
    sum_and_pass(1)

    for i, ee in enumerate((ydn, yup, yfar)):
        ss = ee + 1 - 2 * core
        arrived(tb.at[pl.ds(1, 7), trange(ss)], tsib_sem.at[i])
    for m in (1, 2, 3, 5, 6, 7):
        for h in range(2):
            arrived(dq_slot(m, h), dq_sem.at[m, h])
    gw = None
    for m in range(8):
        add = nn(dqt[m], tb[m])
        gw = add if gw is None else gw + add
    o_gwq[...] = gw.T
    for m in (1, 2, 3):
        for h in range(2):
            arrived(wz.at[m, h], wz_sem.at[m, h])
    mine = d - 4 * xh
    for h in range(2):
        total = wown[h, mine]
        for m in (1, 2, 3):
            total = total + wz[m, h].astype(F32)
        o_gwk[:, hs(h)] = total[0:HD].T
        o_gwv[:, hs(h)] = total[HD:].T

    for copy in sends:
        copy.wait_send()


def hand_over(*refs):
    sources, targets, held, sem = refs[:8], refs[8:16], refs[16:24], refs[24]
    loads = [
        pltpu.make_async_copy(a, b, sem.at[0, i]) for i, (a, b) in enumerate(zip(sources, held))
    ]
    stores = [
        pltpu.make_async_copy(a, b, sem.at[1, i]) for i, (a, b) in enumerate(zip(held, targets))
    ]
    for copy in loads:
        copy.start()
    for copy, store in zip(loads, stores):
        copy.wait()
        store.start()
    for store in stores:
        store.wait()


def body(*args):
    vm, any_ = pl.BlockSpec(memory_space=pltpu.VMEM), pl.BlockSpec(memory_space=pl.ANY)
    shape = jax.ShapeDtypeStruct
    block = (ROWS, ROWS)
    dma = pltpu.SemaphoreType.DMA
    shapes = (
        shape(block, BF16), shape(block, F32), shape(block, F32), shape(block, F32),
        shape(block, BF16), shape((512, ROWS), F32), shape((128, ROWS), F32),
        shape((128, ROWS), F32),
    )
    results = pl.pallas_call(
        kernel,
        out_shape=shapes,
        in_specs=[any_] * 10,
        out_specs=[vm] * 8,
        scratch_shapes=[
            pltpu.VMEM((256, 4096), BF16),
            pltpu.VMEM((4096, 256), BF16),
            pltpu.VMEM((1024, 512), BF16),
            pltpu.VMEM((512, 1024), BF16),
            pltpu.VMEM((4, 256, 256), BF16),
            pltpu.VMEM((256, 256), BF16),
            pltpu.VMEM((8, 2, 256, 1024), BF16),
            pltpu.VMEM((512, 4096), BF16),
            pltpu.VMEM((2, 256, 4096), F32),
            pltpu.VMEM((2, 256, 4096), F32),
            pltpu.VMEM((8, 2, 256, 1), F32),
            pltpu.VMEM((2, 256, 4096), BF16),
            pltpu.VMEM((2, 256, 1), F32),
            pltpu.VMEM((2, 256, 1), F32),
            pltpu.VMEM((2, 256, 128), F32),
            pltpu.VMEM((8, 2, 256, 256), F32),
            pltpu.VMEM((2, 256, 128), F32),
            pltpu.VMEM((2, 256, 128), F32),
            pltpu.VMEM((2, 256, 128), F32),
            pltpu.VMEM((8, 2, 256, 256), BF16),
            pltpu.VMEM((8, 8, 256), F32),
            pltpu.VMEM((8, 256, 512), BF16),
            pltpu.VMEM((8, 256, 256), BF16),
            pltpu.VMEM((2, 4, 256, 128), F32),
            pltpu.VMEM((2, 4, 256, 128), BF16),
            pltpu.VMEM((2, 4, 256, 128), BF16),
            pltpu.VMEM((4, 2, 256, 128), BF16),
            dma((16,)), dma((128,)), dma((8, 4)), dma((8, 4)), dma((8,)), dma((8,)), dma((8,)),
            dma((4,)), dma((3,)), dma((8, 2)), dma((2,)), dma((4, 2)),
        ],
        compiler_params=pltpu.CompilerParams(
            collective_id=0, has_side_effects=True, vmem_limit_bytes=62 << 20
        ),
        name="layer",
    )(*args)
    return tuple(pl.pallas_call(
        hand_over,
        out_shape=shapes,
        in_specs=[any_] * 8,
        out_specs=[any_] * 8,
        scratch_shapes=[pltpu.VMEM(x.shape, x.dtype) for x in shapes] + [dma((2, 8))],
        name="hand_over",
    )(*results))


def solution(mesh):
    placed = (
        P("dec", None), P(None, "enc"), P("enc", None), P(None, "enc"), P(None, "enc"),
    ) + (P("dec", "enc"),) * 5
    return jax.shard_map(
        body, mesh=mesh, in_specs=placed, out_specs=(P("dec", "enc"),) * 8, check_vma=False
    )
```

```python
import jax
import jax.numpy as jnp
from jax import lax
from jax.experimental import pallas as pl
from jax.experimental.pallas import tpu as pltpu
from jax.sharding import PartitionSpec as P

MESH = pl.DeviceIdType.MESH
HD = 128
SCALE = HD ** -0.5
ROWS = 256
F32 = jnp.float32
BF16 = jnp.bfloat16


def nn(a, b):
    return jnp.dot(a, b, preferred_element_type=F32)


def nt(a, b):
    return lax.dot_general(a, b, (((1,), (1,)), ((), ())), preferred_element_type=F32)


def kernel(
    tok_h, wq_h, ctx_h, wk_h, wv_h, sq_h, sk_h, sv_h, gs_h, gc_h,
    o_self, o_dsq, o_dsk, o_dsv, o_cross, o_gwq, o_gwk, o_gwv,
    tok, wq, wkv, wkvt, own, gc, ctx, kvt, wst, dpst, mst, dkvt,
    prob, dscore, cm, cl, cacc, st_top, sst, sm, sl, sacc, blk, stat, tb, dqt, wown, wmine, wpeer, wz,
    lsem, ssem, ctx_sem, sib_sem, blk_sem, stat_sem, tok_sem, tokg_sem, tsib_sem, dq_sem, wp_sem,
    wz_sem,
):
    e = lax.axis_index("enc")
    d = lax.axis_index("dec")
    y, low = e // 4, e % 4
    core = e % 2
    yup = lax.rem(y + 1, 4) * 4 + low
    ydn = lax.rem(y + 3, 4) * 4 + low
    yfar = lax.rem(y + 2, 4) * 4 + low
    sib = e + 1 - 2 * core
    xflip = e + 2 - 4 * ((e // 2) % 2)
    xh = d // 4

    def peer(m):
        out = d
        for bit in (1, 2, 4):
            if m & bit:
                out = out + bit - 2 * bit * ((d // bit) % 2)
        return out

    dev = {
        "yup": (yup, d), "ydn": (ydn, d), "yfar": (yfar, d), "sib": (sib, d),
        "xi": (xflip, d), "xo": (xflip, peer(4)),
    }
    partner = [(e, peer(m)) for m in range(8)]

    barrier = pltpu.get_barrier_semaphore()
    greet = list(dev.values()) + partner[1:]
    for target in greet:
        pl.semaphore_signal(barrier, inc=1, device_id=target, device_id_type=MESH)

    loads = []

    def load(src, dst):
        copy = pltpu.make_async_copy(src, dst, lsem.at[len(loads)])
        copy.start()
        loads.append(copy)
        return copy

    l_own = [load(r, own.at[i]) for i, r in enumerate((sk_h, sv_h, sq_h, gs_h))]
    l_ctx = [load(ctx_h.at[pl.ds(a * 128, 128)], ctx.at[0, a, 0]) for a in range(2)]
    l_wk = load(wk_h, wkv.at[:, pl.ds(0, ROWS)])
    l_wv = load(wv_h, wkv.at[:, pl.ds(ROWS, ROWS)])
    l_gc = load(gc_h, gc)
    l_tok = load(tok_h, tok)
    l_wq = load(wq_h, wq)

    sends = []

    def send(src, dst, rsem, target):
        copy = pltpu.make_async_remote_copy(
            src_ref=src, dst_ref=dst, send_sem=ssem.at[len(sends)], recv_sem=rsem,
            device_id=target, device_id_type=MESH,
        )
        copy.start()
        sends.append(copy)

    def arrived(dst, rsem):
        pltpu.make_async_remote_copy(
            src_ref=dst, dst_ref=dst, send_sem=ssem.at[0], recv_sem=rsem,
            device_id=dev["sib"], device_id_type=MESH,
        ).wait_recv()

    quarter = ROWS // 4

    def part(k, i, side=0):
        return ctx.at[k, i // 2, side, pl.ds(i % 2 * quarter, quarter), :]

    def pass_on(src, k, i, target):
        send(src, part(k, i), ctx_sem.at[k, i], target)

    def got(k, i):
        arrived(part(k, i), ctx_sem.at[k, i])

    def share(k, i):
        send(part(k, i), part(k, i, 1), sib_sem.at[k, i], dev["sib"])

    def shared(k):
        for i in range(4):
            arrived(part(k, i, 1), sib_sem.at[k, i])

    for c in l_own:
        c.wait()
    for c in l_ctx:
        c.wait()
    pl.semaphore_wait(barrier, len(greet))

    def own_block(m):
        bit = (d // (1 if m == 1 else 2 if m < 4 else 4)) % 2
        return own.at[pl.ds(2 * bit, 2)]

    def blk_out(m, slot, src):
        send(src, blk.at[slot], blk_sem.at[slot], partner[m])

    blk_out(4, 4, own_block(4))
    for i in (0, 1):
        pass_on(part(0, i), 1, i, dev["xi"])
        pass_on(part(0, 2 + i), 1, 2 + i, dev["xo"])
        pass_on(part(0, i), 6, i, dev["yup"])
        pass_on(part(0, 2 + i), 2, 2 + i, dev["ydn"])
    for i in range(4):
        share(0, i)
    for i in (0, 1):
        pass_on(part(0, 2 + i), 6, 2 + i, dev["yup"])
        pass_on(part(0, i), 2, i, dev["ydn"])
    for m in (1, 3, 2):
        blk_out(m, m, own_block(m))

    l_wk.wait()
    l_wv.wait()
    wkvt[...] = wkv[...].T
    l_tok.wait()
    l_wq.wait()
    cq = nn(tok[...], wq[...]).astype(BF16)
    cqt = cq.T
    l_gc.wait()
    gcv = gc[...]
    gct = gcv.T

    def hs(h):
        return slice(h * HD, (h + 1) * HD)

    ctx2 = ctx.reshape(16 * ROWS, ctx.shape[4])

    def span(k):
        return slice(k * 2 * ROWS, (k + 1) * 2 * ROWS)

    def lanes(f, x):
        out = x[:, :HD]
        for i in range(1, x.shape[1] // HD):
            out = f(out, x[:, i * HD:(i + 1) * HD])
        return out

    def cross_scores(k, first=False):
        cols = span(k)
        x = ctx2[cols]
        kv = [nt(wkvt[i * ROWS:(i + 1) * ROWS], x).astype(BF16) for i in range(2)]
        for i in range(2):
            kvt[i * ROWS:(i + 1) * ROWS, cols] = kv[i]
        for h in range(2):
            s = nn(cq[:, hs(h)], kv[0][hs(h)]) * SCALE
            wst[h, :, cols] = s
            top = lanes(jnp.maximum, s)
            cm[h] = top if first else jnp.maximum(cm[h], top)
            dpst[h, :, cols] = nn(gcv[:, hs(h)], kv[1][hs(h)])

    def cross_weights(g, chunks):
        for h in range(2):
            top = jnp.max(cm[h], axis=1, keepdims=True)
            mst[g, h] = top
            add_l, add_o = None, None
            for k in chunks:
                cols = span(k)
                w = jnp.exp(wst[h, :, cols] - top)
                wst[h, :, cols] = w
                one_l = lanes(jnp.add, w)
                one_o = nt(w.astype(BF16), kvt[ROWS + h * HD:ROWS + (h + 1) * HD, cols])
                add_l = one_l if add_l is None else add_l + one_l
                add_o = one_o if add_o is None else add_o + one_o
            if g:
                fix = jnp.exp(mst[g - 1, h] - top)
                add_l = add_l + cl[h] * fix
                add_o = add_o + cacc[h] * fix
            cl[h] = add_l
            cacc[h] = add_o

    groups = ((0, 1), (6, 2), (4, 7, 3), (5,))

    row = lax.broadcasted_iota(jnp.int32, (ROWS, ROWS), 0)
    col = lax.broadcasted_iota(jnp.int32, (ROWS, ROWS), 1)

    def xor_slot(p):
        out = 0
        for bit in (1, 2, 4):
            out = out + bit * (((d // bit) + (p // bit)) % 2)
        return out

    def halves(f, x):
        return f(x[:, :HD], x[:, HD:])

    def self_scores(p, carry):
        slot = xor_slot(p)
        for h in range(2):
            s = nt(own[2, :, hs(h)], blk[slot, 0, :, hs(h)]) * SCALE
            sst[slot, h] = s
            sm[h] = jnp.maximum(sm[h], halves(jnp.maximum, s))
        return carry

    def self_weights(p, carry):
        slot = xor_slot(p)
        for h in range(2):
            w = jnp.exp(sst[slot, h] - st_top[h])
            sl[h] += halves(jnp.add, w)
            sacc[h] += nn(w.astype(BF16), blk[slot, 1, :, hs(h)])
        return carry

    shared(0)
    cross_scores(0, True)
    got_up = lambda i: (
        got(6, i),
        pass_on(part(6, i), 4, i, dev["yup"]) if i < 2 else None,
        pass_on(part(6, i), 7, i, dev["xi"] if i < 2 else dev["xo"]),
        share(6, i),
    )
    got_down = lambda i: (
        got(2, i),
        pass_on(part(2, i), 4, i, dev["ydn"]) if i > 1 else None,
        pass_on(part(2, i), 3, i, dev["xi"] if i < 2 else dev["xo"]),
        share(2, i),
    )
    got_up(0)
    got_down(2)
    for h in range(2):
        s = jnp.where(row >= col, nt(own[2, :, hs(h)], own[0, :, hs(h)]) * SCALE, -1e30)
        sst[0, h] = s
        sm[h] = halves(jnp.maximum, s)
    got_up(1)
    got_down(3)
    arrived(blk.at[4], blk_sem.at[4])
    for m in (1, 3, 2):
        blk_out(m, 4 + m, blk.at[4])
    got_up(2)
    got_down(0)
    got_up(3)
    got_down(1)
    shared(6)
    cross_scores(6)
    for i in range(4):
        got(1, i)
        share(1, i)
    shared(2)
    cross_scores(2)
    shared(1)
    cross_scores(1)
    for m in (1, 2, 3):
        arrived(blk.at[m], blk_sem.at[m])
    lax.fori_loop(4 * xh, d, self_scores, 0)
    for i in (0, 1):
        got(7, i)
        pass_on(part(7, i), 5, i, dev["yup"])
        share(7, i)
        got(3, 2 + i)
        pass_on(part(3, 2 + i), 5, 2 + i, dev["ydn"])
        share(3, 2 + i)
    for i in range(4):
        got(4, i)
        share(4, i)
    cross_weights(0, groups[0])
    cross_weights(1, groups[1])
    for h in range(2):
        top = jnp.max(sm[h], axis=1, keepdims=True)
        st_top[h] = top
        w = jnp.exp(sst[0, h] - top)
        sl[h] = halves(jnp.add, w)
        sacc[h] = nn(w.astype(BF16), own[1, :, hs(h)])
    lax.fori_loop(4 * xh, d, self_weights, 0)
    shared(4)
    cross_scores(4)
    for i in (0, 1):
        got(7, 2 + i)
        share(7, 2 + i)
        got(3, i)
        share(3, i)
    shared(7)
    cross_scores(7)
    for i in range(4):
        got(5, i)
        share(5, i)
    shared(3)
    cross_scores(3)
    lane = (y * 2 + core) * 32
    trows = pl.ds(pl.multiple_of(lane, 32), 32)

    def tcols(p):
        return pl.ds(pl.multiple_of(p * 512, 512), 512)

    for m in range(1, 8):
        send(tok.at[trows, tcols(partner[m][1])], tb.at[m, trows], tok_sem.at[m], partner[m])
    l_tb = load(tok.at[:, tcols(d)], tb.at[0])
    cross_weights(2, groups[2])
    shared(5)
    cross_scores(5)
    cross_weights(3, groups[3])

    def weight_part(h, group):
        return nn(dkvt[h], ctx2[:, pl.ds(pl.multiple_of(group * 512, 512), 512)])

    def dq_slot(m, h):
        return dqt.at[m, pl.ds(h * HD, HD), :]

    for h in range(2):
        norm = jnp.sum(cl[h], axis=1, keepdims=True)
        out = (cacc[h] / norm).astype(BF16)
        o_cross[:, hs(h)] = out
        g = gcv[:, hs(h)]
        lse = mst[3, h] + jnp.log(norm)
        delta = jnp.sum(g.astype(F32) * out.astype(F32), axis=1, keepdims=True)
        for i, chunks in enumerate(groups):
            fix = jnp.exp(mst[i, h] - lse)
            for k in chunks:
                cols = span(k)
                p = wst[h, :, cols] * fix
                prob[:, cols] = p.astype(BF16)
                dscore[:, cols] = (p * (dpst[h, :, cols] - delta) * SCALE).astype(BF16)
        dq = nt(dscore[...], kvt[hs(h), :])
        dqt[0, hs(h), :] = dq.astype(BF16).T
        for m in (4, 1, 3, 2):
            send(dq_slot(0, h), dq_slot(m, h), dq_sem.at[m, h], partner[m])
        dkvt[h, 0:HD, :] = nn(cqt[hs(h)], dscore[...]).astype(BF16)
        dkvt[h, HD:, :] = nn(gct[hs(h)], prob[...]).astype(BF16)
        piece = weight_part(h, 1 - xh).astype(BF16)
        for z in range(4):
            wmine[h, z] = piece[:, z * HD:(z + 1) * HD]
        send(wmine.at[h], wpeer.at[h], wp_sem.at[h], partner[4])

    def forward_dq(h):
        arrived(dq_slot(4, h), dq_sem.at[4, h])
        for m in (1, 3, 2):
            send(dq_slot(4, h), dq_slot(4 + m, h), dq_sem.at[4 + m, h], partner[m])

    def sum_and_pass(h):
        arrived(wpeer.at[h], wp_sem.at[h])
        wown[h] = wown[h] + wpeer[h].astype(F32)
        wpeer[h] = wown[h].astype(BF16)
        for m in (1, 3, 2):
            send(
                wpeer.at[h, partner[m][1] - 4 * xh], wz.at[m, h], wz_sem.at[m, h], partner[m]
            )

    def own_weights(h):
        piece = weight_part(h, xh)
        for z in range(4):
            wown[h, z] = piece[:, z * HD:(z + 1) * HD]

    for m in range(1, 8):
        arrived(tb.at[m, trows], tok_sem.at[m])
    l_tb.wait()

    def trange(ee):
        return pl.ds(pl.multiple_of((ee // 4 * 2 + ee % 2) * 32, 32), 32)

    moved = tb.at[pl.ds(1, 7), trows]
    for i, name in enumerate(("yup", "ydn", "yfar", "sib")):
        send(moved, moved, tokg_sem.at[i], dev[name])
    forward_dq(0)
    for m in (5, 6, 7):
        arrived(blk.at[m], blk_sem.at[m])
    lax.fori_loop(0, 4 * xh, self_scores, 0)
    for h in range(2):
        top = jnp.max(sm[h], axis=1, keepdims=True)
        fix = jnp.exp(st_top[h] - top)
        st_top[h] = top
        sl[h] = sl[h] * fix
        sacc[h] = sacc[h] * fix
    lax.fori_loop(0, 4 * xh, self_weights, 0)
    for h in range(2):
        norm = jnp.sum(sl[h], axis=1, keepdims=True)
        out = (sacc[h] / norm).astype(BF16)
        o_self[:, hs(h)] = out
        g = own[3, :, hs(h)]
        lse = st_top[h] + jnp.log(norm)
        delta = jnp.sum(g.astype(F32) * out.astype(F32), axis=1, keepdims=True)
        sm[h] = jnp.broadcast_to(lse, (ROWS, HD))
        sl[h] = jnp.broadcast_to(delta, (ROWS, HD))
        stat[0, 2 * h:2 * h + 1, :] = sm[h].T[0:1]
        stat[0, 2 * h + 1:2 * h + 2, :] = sl[h].T[0:1]
    for m in range(1, 8):
        send(stat.at[0], stat.at[m], stat_sem.at[m], partner[m])
    own_weights(0)
    own_weights(1)
    sum_and_pass(0)
    forward_dq(1)
    def query_grad(h, s, v, k):
        p = jnp.exp(s - sm[h, :, 0:1])
        dp = nt(own[3, :, hs(h)], v)
        return nn((p * (dp - sl[h, :, 0:1]) * SCALE).astype(BF16), k)

    for h in range(2):
        o_dsq[:, hs(h)] = query_grad(h, sst[0, h], own[1, :, hs(h)], own[0, :, hs(h)])

    def self_query(p, carry):
        slot = xor_slot(p)
        for h in range(2):
            o_dsq[:, hs(h)] += query_grad(
                h, sst[slot, h], blk[slot, 1, :, hs(h)], blk[slot, 0, :, hs(h)]
            )
        return carry

    lax.fori_loop(0, d, self_query, 0)

    def key_grad(h, st, q, g, lse, delta):
        p = jnp.exp(st - lse)
        dp = nt(own[1, :, hs(h)], g)
        ds = (p * (dp - delta) * SCALE).astype(BF16)
        return nn(ds, q), nn(p.astype(BF16), g)

    for i, ee in enumerate((ydn, yup, yfar, sib)):
        arrived(tb.at[pl.ds(1, 7), trange(ee)], tokg_sem.at[i])
    for i, ee in enumerate((ydn, yup, yfar)):
        spot = tb.at[pl.ds(1, 7), trange(ee)]
        send(spot, spot, tsib_sem.at[i], dev["sib"])

    for h in range(2):
        q, g = own[2, :, hs(h)], own[3, :, hs(h)]
        st = jnp.where(col >= row, nt(own[0, :, hs(h)], q) * SCALE, -1e30)
        dk, dv = key_grad(h, st, q, g, stat[0, 2 * h:2 * h + 1], stat[0, 2 * h + 1:2 * h + 2])
        o_dsk[:, hs(h)] = dk
        o_dsv[:, hs(h)] = dv
    sum_and_pass(1)
    for m in range(1, 8):
        arrived(stat.at[m], stat_sem.at[m])

    def self_key(p, carry):
        slot = xor_slot(p)
        for h in range(2):
            q, g = blk[slot, 0, :, hs(h)], blk[slot, 1, :, hs(h)]
            st = nt(own[0, :, hs(h)], q) * SCALE
            dk, dv = key_grad(
                h, st, q, g, stat[slot, 2 * h:2 * h + 1], stat[slot, 2 * h + 1:2 * h + 2]
            )
            o_dsk[:, hs(h)] += dk
            o_dsv[:, hs(h)] += dv
        return carry

    lax.fori_loop(d + 1, 8, self_key, 0)
    for i, ee in enumerate((ydn, yup, yfar)):
        ss = ee + 1 - 2 * core
        arrived(tb.at[pl.ds(1, 7), trange(ss)], tsib_sem.at[i])
    for m in (1, 2, 3, 5, 6, 7):
        for h in range(2):
            arrived(dq_slot(m, h), dq_sem.at[m, h])
    gw = None
    for m in range(8):
        add = nn(dqt[m], tb[m])
        gw = add if gw is None else gw + add
    o_gwq[...] = gw.T
    for m in (1, 2, 3):
        for h in range(2):
            arrived(wz.at[m, h], wz_sem.at[m, h])
    mine = d - 4 * xh
    for h in range(2):
        total = wown[h, mine]
        for m in (1, 2, 3):
            total = total + wz[m, h].astype(F32)
        o_gwk[:, hs(h)] = total[0:HD].T
        o_gwv[:, hs(h)] = total[HD:].T

    for copy in sends:
        copy.wait_send()


def hand_over(*refs):
    sources, targets, held, sem = refs[:8], refs[8:16], refs[16:24], refs[24]
    loads = [
        pltpu.make_async_copy(a, b, sem.at[0, i]) for i, (a, b) in enumerate(zip(sources, held))
    ]
    stores = [
        pltpu.make_async_copy(a, b, sem.at[1, i]) for i, (a, b) in enumerate(zip(held, targets))
    ]
    for copy in loads:
        copy.start()
    for copy, store in zip(loads, stores):
        copy.wait()
        store.start()
    for store in stores:
        store.wait()


def body(*args):
    vm, any_ = pl.BlockSpec(memory_space=pltpu.VMEM), pl.BlockSpec(memory_space=pl.ANY)
    shape = jax.ShapeDtypeStruct
    block = (ROWS, ROWS)
    dma = pltpu.SemaphoreType.DMA
    shapes = (
        shape(block, BF16), shape(block, F32), shape(block, F32), shape(block, F32),
        shape(block, BF16), shape((512, ROWS), F32), shape((128, ROWS), F32),
        shape((128, ROWS), F32),
    )
    results = pl.pallas_call(
        kernel,
        out_shape=shapes,
        in_specs=[any_] * 10,
        out_specs=[vm] * 8,
        scratch_shapes=[
            pltpu.VMEM((256, 4096), BF16),
            pltpu.VMEM((4096, 256), BF16),
            pltpu.VMEM((1024, 512), BF16),
            pltpu.VMEM((512, 1024), BF16),
            pltpu.VMEM((4, 256, 256), BF16),
            pltpu.VMEM((256, 256), BF16),
            pltpu.VMEM((8, 2, 2, 128, 1024), BF16),
            pltpu.VMEM((512, 4096), BF16),
            pltpu.VMEM((2, 256, 4096), F32),
            pltpu.VMEM((2, 256, 4096), F32),
            pltpu.VMEM((4, 2, 256, 1), F32),
            pltpu.VMEM((2, 256, 4096), BF16),
            pltpu.VMEM((256, 4096), BF16),
            pltpu.VMEM((256, 4096), BF16),
            pltpu.VMEM((2, 256, 128), F32),
            pltpu.VMEM((2, 256, 128), F32),
            pltpu.VMEM((2, 256, 128), F32),
            pltpu.VMEM((2, 256, 1), F32),
            pltpu.VMEM((8, 2, 256, 256), F32),
            pltpu.VMEM((2, 256, 128), F32),
            pltpu.VMEM((2, 256, 128), F32),
            pltpu.VMEM((2, 256, 128), F32),
            pltpu.VMEM((8, 2, 256, 256), BF16),
            pltpu.VMEM((8, 8, 256), F32),
            pltpu.VMEM((8, 256, 512), BF16),
            pltpu.VMEM((8, 256, 256), BF16),
            pltpu.VMEM((2, 4, 256, 128), F32),
            pltpu.VMEM((2, 4, 256, 128), BF16),
            pltpu.VMEM((2, 4, 256, 128), BF16),
            pltpu.VMEM((4, 2, 256, 128), BF16),
            dma((16,)), dma((128,)), dma((8, 4)), dma((8, 4)), dma((8,)), dma((8,)), dma((8,)),
            dma((4,)), dma((3,)), dma((8, 2)), dma((2,)), dma((4, 2)),
        ],
        compiler_params=pltpu.CompilerParams(
            collective_id=0, has_side_effects=True, vmem_limit_bytes=62 << 20
        ),
        name="layer",
    )(*args)
    return tuple(pl.pallas_call(
        hand_over,
        out_shape=shapes,
        in_specs=[any_] * 8,
        out_specs=[any_] * 8,
        scratch_shapes=[pltpu.VMEM(x.shape, x.dtype) for x in shapes] + [dma((2, 8))],
        name="hand_over",
    )(*results))


def solution(mesh):
    placed = (
        P("dec", None), P(None, "enc"), P("enc", None), P(None, "enc"), P(None, "enc"),
    ) + (P("dec", "enc"),) * 5
    return jax.shard_map(
        body, mesh=mesh, in_specs=placed, out_specs=(P("dec", "enc"),) * 8, check_vma=False
    )
```

```python
import jax
import jax.numpy as jnp
from jax import lax
from jax.experimental import pallas as pl
from jax.experimental.pallas import tpu as pltpu
from jax.sharding import PartitionSpec as P

MESH = pl.DeviceIdType.MESH
HD = 128
SCALE = HD ** -0.5
ROWS = 256
F32 = jnp.float32
BF16 = jnp.bfloat16


def nn(a, b):
    return jnp.dot(a, b, preferred_element_type=F32)


def nt(a, b):
    return lax.dot_general(a, b, (((1,), (1,)), ((), ())), preferred_element_type=F32)


def kernel(
    tok_h, wq_h, ctx_h, wk_h, wv_h, sq_h, sk_h, sv_h, gs_h, gc_h,
    o_self, o_dsq, o_dsk, o_dsv, o_cross, o_gwq, o_gwk, o_gwv,
    tok, wq, wkv, wkvt, own, gc, ctx, kvt, wst, dpst, mst, dkvt,
    prob, dscore, cm, cl, cacc, st_top, sst, sm, sl, sacc, blk, stat, tb, dqt, wown, wmine, wpeer, wz,
    lsem, ssem, ctx_sem, sib_sem, blk_sem, stat_sem, tok_sem, tokg_sem, tsib_sem, dq_sem, wp_sem,
    wz_sem,
):
    e = lax.axis_index("enc")
    d = lax.axis_index("dec")
    y, low = e // 4, e % 4
    core = e % 2
    yup = lax.rem(y + 1, 4) * 4 + low
    ydn = lax.rem(y + 3, 4) * 4 + low
    yfar = lax.rem(y + 2, 4) * 4 + low
    sib = e + 1 - 2 * core
    xflip = e + 2 - 4 * ((e // 2) % 2)
    xh = d // 4

    def peer(m):
        out = d
        for bit in (1, 2, 4):
            if m & bit:
                out = out + bit - 2 * bit * ((d // bit) % 2)
        return out

    dev = {
        "yup": (yup, d), "ydn": (ydn, d), "yfar": (yfar, d), "sib": (sib, d),
        "xi": (xflip, d), "xo": (xflip, peer(4)),
    }
    partner = [(e, peer(m)) for m in range(8)]

    barrier = pltpu.get_barrier_semaphore()
    greet = list(dev.values()) + partner[1:]
    for target in greet:
        pl.semaphore_signal(barrier, inc=1, device_id=target, device_id_type=MESH)

    loads = []

    def load(src, dst):
        copy = pltpu.make_async_copy(src, dst, lsem.at[len(loads)])
        copy.start()
        loads.append(copy)
        return copy

    l_own = [load(r, own.at[i]) for i, r in enumerate((sk_h, sv_h, sq_h, gs_h))]
    l_ctx = [load(ctx_h.at[pl.ds(a * 128, 128)], ctx.at[0, a, 0]) for a in range(2)]
    l_wk = load(wk_h, wkv.at[:, pl.ds(0, ROWS)])
    l_wv = load(wv_h, wkv.at[:, pl.ds(ROWS, ROWS)])
    l_gc = load(gc_h, gc)
    l_tok = load(tok_h, tok)
    l_wq = load(wq_h, wq)

    sends = []

    def send(src, dst, rsem, target):
        copy = pltpu.make_async_remote_copy(
            src_ref=src, dst_ref=dst, send_sem=ssem.at[len(sends)], recv_sem=rsem,
            device_id=target, device_id_type=MESH,
        )
        copy.start()
        sends.append(copy)

    def arrived(dst, rsem):
        pltpu.make_async_remote_copy(
            src_ref=dst, dst_ref=dst, send_sem=ssem.at[0], recv_sem=rsem,
            device_id=dev["sib"], device_id_type=MESH,
        ).wait_recv()

    quarter = ROWS // 4

    def part(k, i, side=0):
        return ctx.at[k, i // 2, side, pl.ds(i % 2 * quarter, quarter), :]

    def pass_on(src, k, i, target):
        send(src, part(k, i), ctx_sem.at[k, i], target)

    def got(k, i):
        arrived(part(k, i), ctx_sem.at[k, i])

    def share(k, i):
        send(part(k, i), part(k, i, 1), sib_sem.at[k, i], dev["sib"])

    def shared(k, pieces=range(4)):
        for i in pieces:
            arrived(part(k, i, 1), sib_sem.at[k, i])

    for c in l_own:
        c.wait()
    for c in l_ctx:
        c.wait()
    pl.semaphore_wait(barrier, len(greet))

    def own_block(m):
        bit = (d // (1 if m == 1 else 2 if m < 4 else 4)) % 2
        return own.at[pl.ds(2 * bit, 2)]

    def blk_out(m, slot, src):
        send(src, blk.at[slot], blk_sem.at[slot], partner[m])

    blk_out(4, 4, own_block(4))
    for i in (0, 1):
        pass_on(part(0, i), 1, i, dev["xi"])
        pass_on(part(0, 2 + i), 1, 2 + i, dev["xo"])
        pass_on(part(0, i), 6, i, dev["yup"])
        pass_on(part(0, 2 + i), 2, 2 + i, dev["ydn"])
    for i in range(4):
        share(0, i)
    for i in (0, 1):
        pass_on(part(0, 2 + i), 6, 2 + i, dev["yup"])
        pass_on(part(0, i), 2, i, dev["ydn"])
    for m in (1, 3, 2):
        blk_out(m, m, own_block(m))

    l_wk.wait()
    l_wv.wait()
    wkvt[...] = wkv[...].T
    l_tok.wait()
    l_wq.wait()
    cq = nn(tok[...], wq[...]).astype(BF16)
    cqt = cq.T
    l_gc.wait()
    gcv = gc[...]
    gct = gcv.T

    def hs(h):
        return slice(h * HD, (h + 1) * HD)

    ctx2 = ctx.reshape(16 * ROWS, ctx.shape[4])

    def span(k):
        return slice(k * 2 * ROWS, (k + 1) * 2 * ROWS)

    def lanes(f, x):
        out = x[:, :HD]
        for i in range(1, x.shape[1] // HD):
            out = f(out, x[:, i * HD:(i + 1) * HD])
        return out

    def cross_scores(k, first=False, half=None):
        cols = span(k)
        if half is not None:
            cols = slice(cols.start + half * ROWS, cols.start + (half + 1) * ROWS)
        x = ctx2[cols]
        kv = [nt(wkvt[i * ROWS:(i + 1) * ROWS], x).astype(BF16) for i in range(2)]
        for i in range(2):
            kvt[i * ROWS:(i + 1) * ROWS, cols] = kv[i]
        for h in range(2):
            s = nn(cq[:, hs(h)], kv[0][hs(h)]) * SCALE
            wst[h, :, cols] = s
            top = lanes(jnp.maximum, s)
            cm[h] = top if first else jnp.maximum(cm[h], top)
            dpst[h, :, cols] = nn(gcv[:, hs(h)], kv[1][hs(h)]) * SCALE

    def cross_weights(g, chunks):
        for h in range(2):
            top = jnp.max(cm[h], axis=1, keepdims=True)
            mst[g, h] = top
            add_l, add_o = None, None
            for k in chunks:
                cols = span(k)
                w = jnp.exp(wst[h, :, cols] - top)
                wst[h, :, cols] = w
                one_l = lanes(jnp.add, w)
                one_o = nt(w.astype(BF16), kvt[ROWS + h * HD:ROWS + (h + 1) * HD, cols])
                add_l = one_l if add_l is None else add_l + one_l
                add_o = one_o if add_o is None else add_o + one_o
            if g:
                fix = jnp.exp(mst[g - 1, h] - top)
                add_l = add_l + cl[h] * fix
                add_o = add_o + cacc[h] * fix
            cl[h] = add_l
            cacc[h] = add_o

    groups = ((0, 1, 6, 2), (4, 7, 3), (5,))

    row = lax.broadcasted_iota(jnp.int32, (ROWS, ROWS), 0)
    col = lax.broadcasted_iota(jnp.int32, (ROWS, ROWS), 1)

    def xor_slot(p):
        out = 0
        for bit in (1, 2, 4):
            out = out + bit * (((d // bit) + (p // bit)) % 2)
        return out

    def halves(f, x):
        return f(x[:, :HD], x[:, HD:])

    def self_scores(p, carry):
        slot = xor_slot(p)
        for h in range(2):
            s = nt(own[2, :, hs(h)], blk[slot, 0, :, hs(h)]) * SCALE
            sst[slot, h] = s
            sm[h] = jnp.maximum(sm[h], halves(jnp.maximum, s))
        return carry

    def self_weights(p, carry):
        slot = xor_slot(p)
        for h in range(2):
            w = jnp.exp(sst[slot, h] - st_top[h])
            sl[h] += halves(jnp.add, w)
            sacc[h] += nn(w.astype(BF16), blk[slot, 1, :, hs(h)])
        return carry

    shared(0)
    cross_scores(0, True)
    got_up = lambda i: (
        got(6, i),
        pass_on(part(6, i), 4, i, dev["yup"]) if i < 2 else None,
        pass_on(part(6, i), 7, i, dev["xi"] if i < 2 else dev["xo"]),
        share(6, i),
    )
    got_down = lambda i: (
        got(2, i),
        pass_on(part(2, i), 4, i, dev["ydn"]) if i > 1 else None,
        pass_on(part(2, i), 3, i, dev["xi"] if i < 2 else dev["xo"]),
        share(2, i),
    )
    got_up(0)
    got_down(2)
    for h in range(2):
        s = jnp.where(row >= col, nt(own[2, :, hs(h)], own[0, :, hs(h)]) * SCALE, -1e30)
        sst[0, h] = s
        sm[h] = halves(jnp.maximum, s)
    got_up(1)
    got_down(3)
    arrived(blk.at[4], blk_sem.at[4])
    for m in (1, 3, 2):
        blk_out(m, 4 + m, blk.at[4])
    shared(6, (0, 1))
    cross_scores(6, half=0)
    got_up(2)
    got_down(0)
    shared(2, (2, 3))
    cross_scores(2, half=1)
    got_up(3)
    got_down(1)
    shared(6, (2, 3))
    cross_scores(6, half=1)
    for i in range(4):
        got(1, i)
        share(1, i)
    shared(2, (0, 1))
    cross_scores(2, half=0)
    shared(1)
    cross_scores(1)
    for m in (1, 2, 3):
        arrived(blk.at[m], blk_sem.at[m])
    lax.fori_loop(4 * xh, d, self_scores, 0)
    for i in (0, 1):
        got(7, i)
        pass_on(part(7, i), 5, i, dev["yup"])
        share(7, i)
        got(3, 2 + i)
        pass_on(part(3, 2 + i), 5, 2 + i, dev["ydn"])
        share(3, 2 + i)
    for i in range(4):
        got(4, i)
        share(4, i)
    cross_weights(0, groups[0])
    shared(4)
    cross_scores(4)
    for h in range(2):
        top = jnp.max(sm[h], axis=1, keepdims=True)
        st_top[h] = top
        w = jnp.exp(sst[0, h] - top)
        sl[h] = halves(jnp.add, w)
        sacc[h] = nn(w.astype(BF16), own[1, :, hs(h)])
    lax.fori_loop(4 * xh, d, self_weights, 0)
    for i in (0, 1):
        got(7, 2 + i)
        share(7, 2 + i)
        got(3, i)
        share(3, i)
    shared(7)
    cross_scores(7)
    for i in range(4):
        got(5, i)
        share(5, i)
    shared(3)
    cross_scores(3)
    lane = (y * 2 + core) * 32
    trows = pl.ds(pl.multiple_of(lane, 32), 32)

    def tcols(p):
        return pl.ds(pl.multiple_of(p * 512, 512), 512)

    for m in range(1, 8):
        send(tok.at[trows, tcols(partner[m][1])], tb.at[m, trows], tok_sem.at[m], partner[m])
    l_tb = load(tok.at[:, tcols(d)], tb.at[0])
    cross_weights(1, groups[1])
    shared(5)
    cross_scores(5)
    cross_weights(2, groups[2])

    def weight_part(h, group):
        return nn(dkvt[h], ctx2[:, pl.ds(pl.multiple_of(group * 512, 512), 512)])

    def dq_slot(m, h):
        return dqt.at[m, pl.ds(h * HD, HD), :]

    def trange(ee):
        return pl.ds(pl.multiple_of((ee // 4 * 2 + ee % 2) * 32, 32), 32)

    def gather_tokens():
        for m in range(1, 8):
            arrived(tb.at[m, trows], tok_sem.at[m])
        l_tb.wait()
        moved = tb.at[pl.ds(1, 7), trows]
        for i, name in enumerate(("yup", "ydn", "yfar", "sib")):
            send(moved, moved, tokg_sem.at[i], dev[name])

    def peer_weights(h):
        piece = weight_part(h, 1 - xh).astype(BF16)
        for z in range(4):
            wmine[h, z] = piece[:, z * HD:(z + 1) * HD]
        for m in (2, 1, 3, 0):
            spot = partner[m][1] - 4 * xh
            send(wmine.at[h, spot], wpeer.at[h, spot], wp_sem.at[h, m], partner[4])

    for h in range(2):
        norm = jnp.sum(cl[h], axis=1, keepdims=True)
        out = (cacc[h] / norm).astype(BF16)
        o_cross[:, hs(h)] = out
        g = gcv[:, hs(h)]
        lse = mst[2, h] + jnp.log(norm)
        delta = jnp.sum(g.astype(F32) * out.astype(F32), axis=1, keepdims=True) * SCALE
        for i, chunks in enumerate(groups):
            fix = jnp.exp(mst[i, h] - lse)
            for k in chunks:
                cols = span(k)
                p = wst[h, :, cols] * fix
                prob[:, cols] = p.astype(BF16)
                dscore[:, cols] = (p * (dpst[h, :, cols] - delta)).astype(BF16)
        dq = nt(dscore[...], kvt[hs(h), :])
        dqt[0, hs(h), :] = dq.astype(BF16).T
        for m in (4, 1, 3, 2):
            send(dq_slot(0, h), dq_slot(m, h), dq_sem.at[m, h], partner[m])
        dkvt[h, 0:HD, :] = nn(cqt[hs(h)], dscore[...]).astype(BF16)
        dkvt[h, HD:, :] = nn(gct[hs(h)], prob[...]).astype(BF16)
        if h == 0:
            peer_weights(0)
            gather_tokens()

    def forward_dq(h):
        arrived(dq_slot(4, h), dq_sem.at[4, h])
        for m in (1, 3, 2):
            send(dq_slot(4, h), dq_slot(4 + m, h), dq_sem.at[4 + m, h], partner[m])

    def sum_and_pass(h):
        for m in (2, 1, 3):
            spot = partner[m][1] - 4 * xh
            arrived(wpeer.at[h, spot], wp_sem.at[h, m])
            wpeer[h, spot] = (wown[h, spot] + wpeer[h, spot].astype(F32)).astype(BF16)
            send(wpeer.at[h, spot], wz.at[m, h], wz_sem.at[m, h], partner[m])

    def own_weights(h):
        piece = weight_part(h, xh)
        for z in range(4):
            wown[h, z] = piece[:, z * HD:(z + 1) * HD]

    forward_dq(0)
    for m in (5, 6, 7):
        arrived(blk.at[m], blk_sem.at[m])
    lax.fori_loop(0, 4 * xh, self_scores, 0)
    for h in range(2):
        top = jnp.max(sm[h], axis=1, keepdims=True)
        fix = jnp.exp(st_top[h] - top)
        st_top[h] = top
        sl[h] = sl[h] * fix
        sacc[h] = sacc[h] * fix
    lax.fori_loop(0, 4 * xh, self_weights, 0)
    for h in range(2):
        norm = jnp.sum(sl[h], axis=1, keepdims=True)
        out = (sacc[h] / norm).astype(BF16)
        o_self[:, hs(h)] = out
        g = own[3, :, hs(h)]
        lse = st_top[h] + jnp.log(norm)
        delta = jnp.sum(g.astype(F32) * out.astype(F32), axis=1, keepdims=True)
        sm[h] = jnp.broadcast_to(lse, (ROWS, HD))
        sl[h] = jnp.broadcast_to(delta, (ROWS, HD))
        stat[0, 2 * h:2 * h + 1, :] = sm[h].T[0:1]
        stat[0, 2 * h + 1:2 * h + 2, :] = sl[h].T[0:1]
    for m in range(1, 8):
        send(stat.at[0], stat.at[m], stat_sem.at[m], partner[m])
    peer_weights(1)
    own_weights(0)
    own_weights(1)
    sum_and_pass(0)
    forward_dq(1)
    def query_grad(h, s, v, k):
        p = jnp.exp(s - sm[h, :, 0:1])
        dp = nt(own[3, :, hs(h)], v)
        return nn((p * (dp - sl[h, :, 0:1]) * SCALE).astype(BF16), k)

    for h in range(2):
        o_dsq[:, hs(h)] = query_grad(h, sst[0, h], own[1, :, hs(h)], own[0, :, hs(h)])

    def self_query(p, carry):
        slot = xor_slot(p)
        for h in range(2):
            o_dsq[:, hs(h)] += query_grad(
                h, sst[slot, h], blk[slot, 1, :, hs(h)], blk[slot, 0, :, hs(h)]
            )
        return carry

    lax.fori_loop(0, d, self_query, 0)

    def key_grad(h, st, q, g, lse, delta):
        p = jnp.exp(st - lse)
        dp = nt(own[1, :, hs(h)], g)
        ds = (p * (dp - delta) * SCALE).astype(BF16)
        return nn(ds, q), nn(p.astype(BF16), g)

    for h in range(2):
        q, g = own[2, :, hs(h)], own[3, :, hs(h)]
        st = jnp.where(col >= row, nt(own[0, :, hs(h)], q) * SCALE, -1e30)
        dk, dv = key_grad(h, st, q, g, stat[0, 2 * h:2 * h + 1], stat[0, 2 * h + 1:2 * h + 2])
        o_dsk[:, hs(h)] = dk
        o_dsv[:, hs(h)] = dv
    sum_and_pass(1)
    for i, ee in enumerate((ydn, yup, yfar, sib)):
        arrived(tb.at[pl.ds(1, 7), trange(ee)], tokg_sem.at[i])
    for i, ee in enumerate((ydn, yup, yfar)):
        spot = tb.at[pl.ds(1, 7), trange(ee)]
        send(spot, spot, tsib_sem.at[i], dev["sib"])

    for m in range(1, 8):
        arrived(stat.at[m], stat_sem.at[m])

    def self_key(p, carry):
        slot = xor_slot(p)
        for h in range(2):
            q, g = blk[slot, 0, :, hs(h)], blk[slot, 1, :, hs(h)]
            st = nt(own[0, :, hs(h)], q) * SCALE
            dk, dv = key_grad(
                h, st, q, g, stat[slot, 2 * h:2 * h + 1], stat[slot, 2 * h + 1:2 * h + 2]
            )
            o_dsk[:, hs(h)] += dk
            o_dsv[:, hs(h)] += dv
        return carry

    lax.fori_loop(d + 1, 8, self_key, 0)
    for i, ee in enumerate((ydn, yup, yfar)):
        ss = ee + 1 - 2 * core
        arrived(tb.at[pl.ds(1, 7), trange(ss)], tsib_sem.at[i])
    for m in (1, 2, 3, 5, 6, 7):
        for h in range(2):
            arrived(dq_slot(m, h), dq_sem.at[m, h])
    gw = None
    for m in range(8):
        add = nn(dqt[m], tb[m])
        gw = add if gw is None else gw + add
    o_gwq[...] = gw.T
    for m in (1, 2, 3):
        for h in range(2):
            arrived(wz.at[m, h], wz_sem.at[m, h])
    mine = d - 4 * xh
    for h in range(2):
        arrived(wpeer.at[h, mine], wp_sem.at[h, 0])
        total = wown[h, mine] + wpeer[h, mine].astype(F32)
        for m in (1, 2, 3):
            total = total + wz[m, h].astype(F32)
        o_gwk[:, hs(h)] = total[0:HD].T
        o_gwv[:, hs(h)] = total[HD:].T

    for copy in sends:
        copy.wait_send()


def hand_over(*refs):
    sources, targets, held, sem = refs[:8], refs[8:16], refs[16:24], refs[24]
    loads = [
        pltpu.make_async_copy(a, b, sem.at[0, i]) for i, (a, b) in enumerate(zip(sources, held))
    ]
    stores = [
        pltpu.make_async_copy(a, b, sem.at[1, i]) for i, (a, b) in enumerate(zip(held, targets))
    ]
    for copy in loads:
        copy.start()
    for copy, store in zip(loads, stores):
        copy.wait()
        store.start()
    for store in stores:
        store.wait()


def body(*args):
    vm, any_ = pl.BlockSpec(memory_space=pltpu.VMEM), pl.BlockSpec(memory_space=pl.ANY)
    shape = jax.ShapeDtypeStruct
    block = (ROWS, ROWS)
    dma = pltpu.SemaphoreType.DMA
    shapes = (
        shape(block, BF16), shape(block, F32), shape(block, F32), shape(block, F32),
        shape(block, BF16), shape((512, ROWS), F32), shape((128, ROWS), F32),
        shape((128, ROWS), F32),
    )
    results = pl.pallas_call(
        kernel,
        out_shape=shapes,
        in_specs=[any_] * 10,
        out_specs=[vm] * 8,
        scratch_shapes=[
            pltpu.VMEM((256, 4096), BF16),
            pltpu.VMEM((4096, 256), BF16),
            pltpu.VMEM((1024, 512), BF16),
            pltpu.VMEM((512, 1024), BF16),
            pltpu.VMEM((4, 256, 256), BF16),
            pltpu.VMEM((256, 256), BF16),
            pltpu.VMEM((8, 2, 2, 128, 1024), BF16),
            pltpu.VMEM((512, 4096), BF16),
            pltpu.VMEM((2, 256, 4096), F32),
            pltpu.VMEM((2, 256, 4096), F32),
            pltpu.VMEM((4, 2, 256, 1), F32),
            pltpu.VMEM((2, 256, 4096), BF16),
            pltpu.VMEM((256, 4096), BF16),
            pltpu.VMEM((256, 4096), BF16),
            pltpu.VMEM((2, 256, 128), F32),
            pltpu.VMEM((2, 256, 128), F32),
            pltpu.VMEM((2, 256, 128), F32),
            pltpu.VMEM((2, 256, 1), F32),
            pltpu.VMEM((8, 2, 256, 256), F32),
            pltpu.VMEM((2, 256, 128), F32),
            pltpu.VMEM((2, 256, 128), F32),
            pltpu.VMEM((2, 256, 128), F32),
            pltpu.VMEM((8, 2, 256, 256), BF16),
            pltpu.VMEM((8, 8, 256), F32),
            pltpu.VMEM((8, 256, 512), BF16),
            pltpu.VMEM((8, 256, 256), BF16),
            pltpu.VMEM((2, 4, 256, 128), F32),
            pltpu.VMEM((2, 4, 256, 128), BF16),
            pltpu.VMEM((2, 4, 256, 128), BF16),
            pltpu.VMEM((4, 2, 256, 128), BF16),
            dma((16,)), dma((128,)), dma((8, 4)), dma((8, 4)), dma((8,)), dma((8,)), dma((8,)),
            dma((4,)), dma((3,)), dma((8, 2)), dma((2, 4)), dma((4, 2)),
        ],
        compiler_params=pltpu.CompilerParams(
            collective_id=0, has_side_effects=True, vmem_limit_bytes=62 << 20
        ),
        name="layer",
    )(*args)
    return tuple(pl.pallas_call(
        hand_over,
        out_shape=shapes,
        in_specs=[any_] * 8,
        out_specs=[any_] * 8,
        scratch_shapes=[pltpu.VMEM(x.shape, x.dtype) for x in shapes] + [dma((2, 8))],
        name="hand_over",
    )(*results))


def solution(mesh):
    placed = (
        P("dec", None), P(None, "enc"), P("enc", None), P(None, "enc"), P(None, "enc"),
    ) + (P("dec", "enc"),) * 5
    return jax.shard_map(
        body, mesh=mesh, in_specs=placed, out_specs=(P("dec", "enc"),) * 8, check_vma=False
    )
```

```python
import math

import jax
import jax.numpy as jnp
from jax import lax
from jax.experimental import pallas as pl
from jax.experimental.pallas import tpu as pltpu
from jax.sharding import PartitionSpec as P

MESH = pl.DeviceIdType.MESH
HD = 128
SCALE = HD ** -0.5
ROWS = 256
F32 = jnp.float32
BF16 = jnp.bfloat16


def nn(a, b):
    return jnp.dot(a, b, preferred_element_type=F32)


def nt(a, b):
    return lax.dot_general(a, b, (((1,), (1,)), ((), ())), preferred_element_type=F32)


def kernel(
    tok_h, wq_h, ctx_h, wk_h, wv_h, sq_h, sk_h, sv_h, gs_h, gc_h,
    r_self, r_dsq, r_dsk, r_dsv, r_cross, r_gwq, r_gwk, r_gwv,
    o_self, o_dsq, o_dsk, o_dsv, o_cross, o_gwq, o_gwk, o_gwv,
    tok, wq, wkv, wkvt, own, gc, ctx, kvt, wst, dpst, mst, dkvt,
    prob, dscore, cm, cl, cacc, st_top, sst, sm, sl, sacc, blk, stat, tb, dqt, wown, wmine, wpeer, wz,
    lsem, ssem, ctx_sem, sib_sem, blk_sem, stat_sem, tok_sem, dq_sem, wp_sem, wz_sem, out_sem,
):
    e = lax.axis_index("enc")
    d = lax.axis_index("dec")
    y, low = e // 4, e % 4
    core = e % 2
    yup = lax.rem(y + 1, 4) * 4 + low
    ydn = lax.rem(y + 3, 4) * 4 + low
    yfar = lax.rem(y + 2, 4) * 4 + low
    sib = e + 1 - 2 * core
    xflip = e + 2 - 4 * ((e // 2) % 2)
    xh = d // 4

    def peer(m):
        out = d
        for bit in (1, 2, 4):
            if m & bit:
                out = out + bit - 2 * bit * ((d // bit) % 2)
        return out

    dev = {
        "yup": (yup, d), "ydn": (ydn, d), "yfar": (yfar, d), "sib": (sib, d),
        "xi": (xflip, d), "xo": (xflip, peer(4)),
    }
    partner = [(e, peer(m)) for m in range(8)]

    barrier = pltpu.get_barrier_semaphore()
    greet = list(dev.values()) + partner[1:]
    for target in greet:
        pl.semaphore_signal(barrier, inc=1, device_id=target, device_id_type=MESH)

    loads = []

    def load(src, dst):
        copy = pltpu.make_async_copy(src, dst, lsem.at[len(loads)])
        copy.start()
        loads.append(copy)
        return copy

    l_own = [load(r, own.at[i]) for i, r in enumerate((sk_h, sv_h, sq_h, gs_h))]
    l_ctx = [load(ctx_h.at[pl.ds(a * 128, 128)], ctx.at[0, a, 0]) for a in range(2)]
    l_wk = load(wk_h, wkv.at[:, pl.ds(0, ROWS)])
    l_wv = load(wv_h, wkv.at[:, pl.ds(ROWS, ROWS)])
    l_gc = load(gc_h, gc)
    l_tok = load(tok_h, tok)
    l_wq = load(wq_h, wq)

    leaving = []

    def store(src, dst):
        copy = pltpu.make_async_copy(src, dst, out_sem.at[len(leaving)])
        copy.start()
        leaving.append(copy)

    sent = {}

    def send(kind, src, dst, rsem, target):
        group = list(sent).index(kind) if kind in sent else len(sent)
        pltpu.make_async_remote_copy(
            src_ref=src, dst_ref=dst, send_sem=ssem.at[group], recv_sem=rsem,
            device_id=target, device_id_type=MESH,
        ).start()
        sent[kind] = sent.get(kind, 0) + math.prod(src.shape)

    def sent_all(kind, whole):
        assert sent[kind] == math.prod(whole.shape), kind
        pltpu.make_async_remote_copy(
            src_ref=whole, dst_ref=whole, send_sem=ssem.at[list(sent).index(kind)],
            recv_sem=lsem.at[0], device_id=dev["sib"], device_id_type=MESH,
        ).wait_send()

    def arrived(dst, rsem):
        pltpu.make_async_remote_copy(
            src_ref=dst, dst_ref=dst, send_sem=ssem.at[0], recv_sem=rsem,
            device_id=dev["sib"], device_id_type=MESH,
        ).wait_recv()

    quarter = ROWS // 4
    slots = {}

    def slot_sem(k, i):
        alone = k in (2, 6) or (k, i) in ((7, 0), (7, 1), (3, 2), (3, 3))
        return ctx_sem.at[slots.setdefault((k, i if alone else i // 2 * 2), len(slots))]

    def part(k, i, side=0):
        return ctx.at[k, i // 2, side, pl.ds(i % 2 * quarter, quarter), :]

    def pair(k, a, side=0):
        return ctx.at[k, a, side]

    def pass_on(src, k, i, target):
        send("context", src, part(k, i), slot_sem(k, i), target)

    def got(k, i):
        arrived(part(k, i), slot_sem(k, i))

    def got_pair(k, a):
        arrived(pair(k, a), slot_sem(k, 2 * a))
        share_pair(k, a)

    def share(k, i):
        send("share", part(k, i), part(k, i, 1), sib_sem.at[2 * k + i // 2], dev["sib"])

    def share_pair(k, a):
        send("share", pair(k, a), pair(k, a, 1), sib_sem.at[2 * k + a], dev["sib"])

    def shared(k, halves_=(0, 1)):
        for a in halves_:
            arrived(pair(k, a, 1), sib_sem.at[2 * k + a])

    for c in l_own:
        c.wait()
    for c in l_ctx:
        c.wait()
    pl.semaphore_wait(barrier, len(greet))

    def own_block(m):
        bit = (d // (1 if m == 1 else 2 if m < 4 else 4)) % 2
        return own.at[pl.ds(2 * bit, 2)]

    def blk_out(m, slot, src):
        spot = 1 if slot == 4 else 0 if slot < 4 else 2
        send("block", src, blk.at[slot], blk_sem.at[spot], partner[m])

    blk_out(4, 4, own_block(4))
    for i in (0, 1):
        send("context", pair(0, i), pair(1, i), slot_sem(1, 2 * i), dev["xo" if i else "xi"])
        pass_on(part(0, i), 6, i, dev["yup"])
        pass_on(part(0, 2 + i), 2, 2 + i, dev["ydn"])
    for a in range(2):
        share_pair(0, a)
    for i in (0, 1):
        pass_on(part(0, 2 + i), 6, 2 + i, dev["yup"])
        pass_on(part(0, i), 2, i, dev["ydn"])
    for m in (1, 3, 2):
        blk_out(m, m, own_block(m))

    l_wk.wait()
    l_wv.wait()
    wkvt[...] = wkv[...].T
    l_tok.wait()
    l_wq.wait()
    cq = nn(tok[...], wq[...]).astype(BF16)
    cqt = cq.T
    l_gc.wait()
    gcv = gc[...]
    gct = gcv.T

    def hs(h):
        return slice(h * HD, (h + 1) * HD)

    ctx2 = ctx.reshape(16 * ROWS, ctx.shape[4])

    def span(k):
        return slice(k * 2 * ROWS, (k + 1) * 2 * ROWS)

    def lanes(f, x):
        out = x[:, :HD]
        for i in range(1, x.shape[1] // HD):
            out = f(out, x[:, i * HD:(i + 1) * HD])
        return out

    def unit(k, half):
        return slice((2 * k + half) * ROWS, (2 * k + half + 1) * ROWS)

    def cross_scores(k, first=False, half=None):
        cols = span(k) if half is None else unit(k, half)
        x = ctx2[cols]
        kv = [nt(wkvt[i * ROWS:(i + 1) * ROWS], x).astype(BF16) for i in range(2)]
        for i in range(2):
            kvt[i * ROWS:(i + 1) * ROWS, cols] = kv[i]
        for h in range(2):
            s = nn(cq[:, hs(h)], kv[0][hs(h)]) * SCALE
            wst[h, :, cols] = s
            top = lanes(jnp.maximum, s)
            cm[h] = top if first else jnp.maximum(cm[h], top)
            dpst[h, :, cols] = nn(gcv[:, hs(h)], kv[1][hs(h)]) * SCALE

    def cross_weights(g, chunks):
        for h in range(2):
            top = jnp.max(cm[h], axis=1, keepdims=True)
            mst[g, h] = top
            add_l, add_o = None, None
            for cols in chunks:
                w = jnp.exp(wst[h, :, cols] - top)
                wst[h, :, cols] = w
                one_l = lanes(jnp.add, w)
                one_o = nt(w.astype(BF16), kvt[ROWS + h * HD:ROWS + (h + 1) * HD, cols])
                add_l = one_l if add_l is None else add_l + one_l
                add_o = one_o if add_o is None else add_o + one_o
            if g:
                fix = jnp.exp(mst[g - 1, h] - top)
                add_l = add_l + cl[h] * fix
                add_o = add_o + cacc[h] * fix
            cl[h] = add_l
            cacc[h] = add_o

    groups = (
        (span(0), span(1), span(6), span(2)),
        (span(4), unit(7, 0), unit(3, 1)),
        (unit(7, 1), unit(3, 0), span(5)),
    )

    row = lax.broadcasted_iota(jnp.int32, (ROWS, ROWS), 0)
    col = lax.broadcasted_iota(jnp.int32, (ROWS, ROWS), 1)

    def xor_slot(p):
        out = 0
        for bit in (1, 2, 4):
            out = out + bit * (((d // bit) + (p // bit)) % 2)
        return out

    def halves(f, x):
        return f(x[:, :HD], x[:, HD:])

    def self_scores(p, carry):
        slot = xor_slot(p)
        for h in range(2):
            s = nt(own[2, :, hs(h)], blk[slot, 0, :, hs(h)]) * SCALE
            sst[slot, h] = s
            sm[h] = jnp.maximum(sm[h], halves(jnp.maximum, s))
        return carry

    def self_weights(p, carry):
        slot = xor_slot(p)
        for h in range(2):
            w = jnp.exp(sst[slot, h] - st_top[h])
            sl[h] += halves(jnp.add, w)
            sacc[h] += nn(w.astype(BF16), blk[slot, 1, :, hs(h)])
        return carry

    shared(0)
    cross_scores(0, True)
    got_up = lambda i: (
        got(6, i),
        pass_on(part(6, i), 4, i, dev["yup"]) if i < 2 else None,
        pass_on(part(6, i), 7, i, dev["xi"] if i < 2 else dev["xo"]),
        share(6, i),
    )
    got_down = lambda i: (
        got(2, i),
        pass_on(part(2, i), 4, i, dev["ydn"]) if i > 1 else None,
        pass_on(part(2, i), 3, i, dev["xi"] if i < 2 else dev["xo"]),
        share(2, i),
    )
    got_up(0)
    got_down(2)
    for h in range(2):
        s = jnp.where(row >= col, nt(own[2, :, hs(h)], own[0, :, hs(h)]) * SCALE, -1e30)
        sst[0, h] = s
        sm[h] = halves(jnp.maximum, s)
    got_up(1)
    got_down(3)
    arrived(blk.at[4], blk_sem.at[1])
    for m in (1, 3, 2):
        blk_out(m, 4 + m, blk.at[4])
    shared(6, (0,))
    cross_scores(6, half=0)
    got_up(2)
    got_down(0)
    shared(2, (1,))
    cross_scores(2, half=1)
    got_up(3)
    got_down(1)
    shared(6, (1,))
    cross_scores(6, half=1)
    for a in range(2):
        got_pair(1, a)
    shared(2, (0,))
    cross_scores(2, half=0)
    shared(1)
    cross_scores(1)
    arrived(blk.at[pl.ds(1, 3)], blk_sem.at[0])
    lax.fori_loop(4 * xh, d, self_scores, 0)
    for i in (0, 1):
        got(7, i)
        pass_on(part(7, i), 5, i, dev["yup"])
        share(7, i)
        got(3, 2 + i)
        pass_on(part(3, 2 + i), 5, 2 + i, dev["ydn"])
        share(3, 2 + i)
    for a in range(2):
        got_pair(4, a)
    cross_weights(0, groups[0])
    shared(7, (0,))
    cross_scores(7, half=0)
    shared(3, (1,))
    cross_scores(3, half=1)
    shared(4)
    cross_scores(4)
    cross_weights(1, groups[1])
    got_pair(7, 1)
    got_pair(3, 0)
    for h in range(2):
        top = jnp.max(sm[h], axis=1, keepdims=True)
        st_top[h] = top
        w = jnp.exp(sst[0, h] - top)
        sl[h] = halves(jnp.add, w)
        sacc[h] = nn(w.astype(BF16), own[1, :, hs(h)])
    lax.fori_loop(4 * xh, d, self_weights, 0)
    for a in range(2):
        got_pair(5, a)
    shared(7, (1,))
    cross_scores(7, half=1)
    shared(3, (0,))
    cross_scores(3, half=0)
    lane = (y * 2 + core) * 32
    trows = pl.ds(pl.multiple_of(lane, 32), 32)

    def tcols(p):
        return pl.ds(pl.multiple_of(p * 512, 512), 512)

    for m in range(1, 8):
        send("columns", tok.at[trows, tcols(partner[m][1])], tb.at[m, trows], tok_sem.at[0], partner[m])
    l_tb = load(tok.at[:, tcols(d)], tb.at[0])
    shared(5)
    cross_scores(5)
    cross_weights(2, groups[2])

    def weight_part(h, group):
        return nn(dkvt[h], ctx2[:, pl.ds(pl.multiple_of(group * 512, 512), 512)])

    def dq_slot(m, h):
        return dqt.at[m, pl.ds(h * HD, HD), :]

    def trange(ee):
        return pl.ds(pl.multiple_of((ee // 4 * 2 + ee % 2) * 32, 32), 32)

    def gather_tokens():
        moved = tb.at[pl.ds(1, 7), trows]
        arrived(moved, tok_sem.at[0])
        l_tb.wait()
        for name in ("yup", "ydn", "yfar", "sib"):
            send("rows", moved, moved, tok_sem.at[1], dev[name])

    def send_pieces(h, pieces):
        for m in pieces:
            spot = partner[m][1] - 4 * xh
            send("peer", wmine.at[h, spot], wpeer.at[h, spot], wp_sem.at[h, m], partner[4])

    def peer_weights(h):
        piece = weight_part(h, 1 - xh).astype(BF16)
        for z in range(4):
            wmine[h, z] = piece[:, z * HD:(z + 1) * HD]
        send_pieces(h, (2, 1, 3))

    for h in range(2):
        norm = jnp.sum(cl[h], axis=1, keepdims=True)
        out = (cacc[h] / norm).astype(BF16)
        o_cross[:, hs(h)] = out
        g = gcv[:, hs(h)]
        lse = mst[2, h] + jnp.log(norm)
        delta = jnp.sum(g.astype(F32) * out.astype(F32), axis=1, keepdims=True) * SCALE
        for i, chunks in enumerate(groups):
            fix = jnp.exp(mst[i, h] - lse)
            for cols in chunks:
                p = wst[h, :, cols] * fix
                prob[:, cols] = p.astype(BF16)
                dscore[:, cols] = (p * (dpst[h, :, cols] - delta)).astype(BF16)
        dq = nt(dscore[...], kvt[hs(h), :])
        dqt[0, hs(h), :] = dq.astype(BF16).T
        for m in (4, 1, 3, 2):
            send("dq", dq_slot(0, h), dq_slot(m, h), dq_sem.at[h if m == 4 else 2], partner[m])
        dkvt[h, 0:HD, :] = nn(cqt[hs(h)], dscore[...]).astype(BF16)
        dkvt[h, HD:, :] = nn(gct[hs(h)], prob[...]).astype(BF16)
        if h == 0:
            peer_weights(0)
            gather_tokens()

    def forward_dq(h):
        arrived(dq_slot(4, h), dq_sem.at[h])
        for m in (1, 3, 2):
            send("dq", dq_slot(4, h), dq_slot(4 + m, h), dq_sem.at[3], partner[m])

    def sum_and_pass(h):
        for m in (2, 1, 3):
            spot = partner[m][1] - 4 * xh
            arrived(wpeer.at[h, spot], wp_sem.at[h, m])
            wpeer[h, spot] = (wown[h, spot] + wpeer[h, spot].astype(F32)).astype(BF16)
            send("sum", wpeer.at[h, spot], wz.at[m, h], wz_sem.at[0], partner[m])

    def own_weights(h):
        piece = weight_part(h, xh)
        for z in range(4):
            wown[h, z] = piece[:, z * HD:(z + 1) * HD]

    peer_weights(1)
    forward_dq(0)
    own_weights(0)
    arrived(blk.at[pl.ds(5, 3)], blk_sem.at[2])
    lax.fori_loop(0, 4 * xh, self_scores, 0)
    for h in range(2):
        top = jnp.max(sm[h], axis=1, keepdims=True)
        fix = jnp.exp(st_top[h] - top)
        st_top[h] = top
        sl[h] = sl[h] * fix
        sacc[h] = sacc[h] * fix
    lax.fori_loop(0, 4 * xh, self_weights, 0)
    for h in range(2):
        norm = jnp.sum(sl[h], axis=1, keepdims=True)
        out = (sacc[h] / norm).astype(BF16)
        o_self[:, hs(h)] = out
        g = own[3, :, hs(h)]
        lse = st_top[h] + jnp.log(norm)
        delta = jnp.sum(g.astype(F32) * out.astype(F32), axis=1, keepdims=True)
        sm[h] = jnp.broadcast_to(lse, (ROWS, HD))
        sl[h] = jnp.broadcast_to(delta, (ROWS, HD))
        stat[0, 2 * h:2 * h + 1, :] = sm[h].T[0:1]
        stat[0, 2 * h + 1:2 * h + 2, :] = sl[h].T[0:1]
    store(o_self, r_self)
    store(o_cross, r_cross)
    for m in range(1, 8):
        send("stat", stat.at[0], stat.at[m], stat_sem.at[0], partner[m])
    for h in range(2):
        send_pieces(h, (0,))
    sum_and_pass(0)
    own_weights(1)
    forward_dq(1)
    def query_grad(h, s, v, k):
        p = jnp.exp(s - sm[h, :, 0:1])
        dp = nt(own[3, :, hs(h)], v)
        return nn((p * (dp - sl[h, :, 0:1]) * SCALE).astype(BF16), k)

    for h in range(2):
        o_dsq[:, hs(h)] = query_grad(h, sst[0, h], own[1, :, hs(h)], own[0, :, hs(h)])

    def self_query(p, carry):
        slot = xor_slot(p)
        for h in range(2):
            o_dsq[:, hs(h)] += query_grad(
                h, sst[slot, h], blk[slot, 1, :, hs(h)], blk[slot, 0, :, hs(h)]
            )
        return carry

    lax.fori_loop(0, d, self_query, 0)
    store(o_dsq, r_dsq)

    sum_and_pass(1)
    arrived(tb.at[pl.ds(1, 7), pl.ds(0, 128)], tok_sem.at[1])
    for ee in (ydn, yup, yfar):
        spot = tb.at[pl.ds(1, 7), trange(ee)]
        send("rows", spot, spot, tok_sem.at[2], dev["sib"])

    def key_grad(h, st, q, g, lse, delta):
        p = jnp.exp(st - lse)
        dp = nt(own[1, :, hs(h)], g)
        ds = (p * (dp - delta) * SCALE).astype(BF16)
        return nn(ds, q), nn(p.astype(BF16), g)

    for h in range(2):
        q, g = own[2, :, hs(h)], own[3, :, hs(h)]
        st = jnp.where(col >= row, nt(own[0, :, hs(h)], q) * SCALE, -1e30)
        dk, dv = key_grad(h, st, q, g, stat[0, 2 * h:2 * h + 1], stat[0, 2 * h + 1:2 * h + 2])
        o_dsk[:, hs(h)] = dk
        o_dsv[:, hs(h)] = dv
    arrived(stat.at[pl.ds(1, 7)], stat_sem.at[0])

    def self_key(p, carry):
        slot = xor_slot(p)
        for h in range(2):
            q, g = blk[slot, 0, :, hs(h)], blk[slot, 1, :, hs(h)]
            st = nt(own[0, :, hs(h)], q) * SCALE
            dk, dv = key_grad(
                h, st, q, g, stat[slot, 2 * h:2 * h + 1], stat[slot, 2 * h + 1:2 * h + 2]
            )
            o_dsk[:, hs(h)] += dk
            o_dsv[:, hs(h)] += dv
        return carry

    lax.fori_loop(d + 1, 8, self_key, 0)
    store(o_dsk, r_dsk)
    store(o_dsv, r_dsv)
    arrived(tb.at[pl.ds(1, 7), pl.ds(0, 96)], tok_sem.at[2])
    arrived(dqt.at[pl.ds(1, 3)], dq_sem.at[2])
    arrived(dqt.at[pl.ds(5, 3)], dq_sem.at[3])
    gw = None
    for m in range(8):
        add = nn(dqt[m], tb[m])
        gw = add if gw is None else gw + add
    o_gwq[...] = gw.T
    store(o_gwq, r_gwq)
    arrived(wz.at[pl.ds(1, 3)], wz_sem.at[0])
    mine = d - 4 * xh
    for h in range(2):
        arrived(wpeer.at[h, mine], wp_sem.at[h, 0])
        total = wown[h, mine] + wpeer[h, mine].astype(F32)
        for m in (1, 2, 3):
            total = total + wz[m, h].astype(F32)
        o_gwk[:, hs(h)] = total[0:HD].T
        o_gwv[:, hs(h)] = total[HD:].T
    store(o_gwk, r_gwk)
    store(o_gwv, r_gwv)

    sent_all("context", ctx.at[pl.ds(0, 7), :, 0])
    sent_all("share", ctx.at[:, :, 0])
    sent_all("block", blk.at[pl.ds(0, 7)])
    sent_all("columns", tb.at[pl.ds(1, 7), pl.ds(0, 32)])
    sent_all("rows", tb.at[pl.ds(1, 7), pl.ds(0, 224)])
    sent_all("peer", wmine)
    sent_all("dq", dqt.at[pl.ds(0, 7)])
    sent_all("sum", wz.at[pl.ds(1, 3)])
    sent_all("stat", stat.at[pl.ds(1, 7)])
    for copy in leaving:
        copy.wait()


def hand_over(*refs):
    sources, targets, held, sem = refs[:8], refs[8:16], refs[16:24], refs[24]
    loads = [
        pltpu.make_async_copy(a, b, sem.at[0, i]) for i, (a, b) in enumerate(zip(sources, held))
    ]
    stores = [
        pltpu.make_async_copy(a, b, sem.at[1, i]) for i, (a, b) in enumerate(zip(held, targets))
    ]
    for copy in loads:
        copy.start()
    for copy, store in zip(loads, stores):
        copy.wait()
        store.start()
    for store in stores:
        store.wait()


def body(*args):
    any_ = pl.BlockSpec(memory_space=pl.ANY)
    shape = jax.ShapeDtypeStruct
    block = (ROWS, ROWS)
    dma = pltpu.SemaphoreType.DMA
    shapes = (
        shape(block, BF16), shape(block, F32), shape(block, F32), shape(block, F32),
        shape(block, BF16), shape((512, ROWS), F32), shape((128, ROWS), F32),
        shape((128, ROWS), F32),
    )
    results = pl.pallas_call(
        kernel,
        out_shape=shapes,
        in_specs=[any_] * 10,
        out_specs=[any_] * 8,
        scratch_shapes=[pltpu.VMEM(x.shape, x.dtype) for x in shapes] + [
            pltpu.VMEM((256, 4096), BF16),
            pltpu.VMEM((4096, 256), BF16),
            pltpu.VMEM((1024, 512), BF16),
            pltpu.VMEM((512, 1024), BF16),
            pltpu.VMEM((4, 256, 256), BF16),
            pltpu.VMEM((256, 256), BF16),
            pltpu.VMEM((8, 2, 2, 128, 1024), BF16),
            pltpu.VMEM((512, 4096), BF16),
            pltpu.VMEM((2, 256, 4096), F32),
            pltpu.VMEM((2, 256, 4096), F32),
            pltpu.VMEM((4, 2, 256, 1), F32),
            pltpu.VMEM((2, 256, 4096), BF16),
            pltpu.VMEM((256, 4096), BF16),
            pltpu.VMEM((256, 4096), BF16),
            pltpu.VMEM((2, 256, 128), F32),
            pltpu.VMEM((2, 256, 128), F32),
            pltpu.VMEM((2, 256, 128), F32),
            pltpu.VMEM((2, 256, 1), F32),
            pltpu.VMEM((8, 2, 256, 256), F32),
            pltpu.VMEM((2, 256, 128), F32),
            pltpu.VMEM((2, 256, 128), F32),
            pltpu.VMEM((2, 256, 128), F32),
            pltpu.VMEM((8, 2, 256, 256), BF16),
            pltpu.VMEM((8, 8, 256), F32),
            pltpu.VMEM((8, 256, 512), BF16),
            pltpu.VMEM((8, 256, 256), BF16),
            pltpu.VMEM((2, 4, 256, 128), F32),
            pltpu.VMEM((2, 4, 256, 128), BF16),
            pltpu.VMEM((2, 4, 256, 128), BF16),
            pltpu.VMEM((4, 2, 256, 128), BF16),
            dma((12,)), dma((9,)), dma((20,)), dma((16,)), dma((3,)), dma((1,)), dma((3,)),
            dma((4,)), dma((2, 4)), dma((1,)), dma((8,)),
        ],
        compiler_params=pltpu.CompilerParams(
            collective_id=0, has_side_effects=True, vmem_limit_bytes=62 << 20
        ),
        name="layer",
    )(*args)
    return tuple(pl.pallas_call(
        hand_over,
        out_shape=shapes,
        in_specs=[any_] * 8,
        out_specs=[any_] * 8,
        scratch_shapes=[pltpu.VMEM(x.shape, x.dtype) for x in shapes] + [dma((2, 8))],
        name="hand_over",
    )(*results))


def solution(mesh):
    placed = (
        P("dec", None), P(None, "enc"), P("enc", None), P(None, "enc"), P(None, "enc"),
    ) + (P("dec", "enc"),) * 5
    return jax.shard_map(
        body, mesh=mesh, in_specs=placed, out_specs=(P("dec", "enc"),) * 8, check_vma=False
    )
```

```python
import math

import jax
import jax.numpy as jnp
from jax import lax
from jax.experimental import pallas as pl
from jax.experimental.pallas import tpu as pltpu
from jax.sharding import PartitionSpec as P

MESH = pl.DeviceIdType.MESH
HD = 128
SCALE = HD ** -0.5
ROWS = 256
F32 = jnp.float32
BF16 = jnp.bfloat16


def nn(a, b):
    return jnp.dot(a, b, preferred_element_type=F32)


def nt(a, b):
    return lax.dot_general(a, b, (((1,), (1,)), ((), ())), preferred_element_type=F32)


def kernel(
    tok_h, wq_h, ctx_h, wk_h, wv_h, sq_h, sk_h, sv_h, gs_h, gc_h,
    r_self, r_dsq, r_dsk, r_dsv, r_cross, r_gwq, r_gwk, r_gwv,
    o_self, o_dsq, o_dsk, o_dsv, o_cross, o_gwq, o_gwk, o_gwv,
    tok, wq, wkv, wkvt, own, gc, ctx, kvt, wst, dpst, mst, dkvt,
    prob, dscore, cm, cl, cacc, st_top, sst, sm, sl, sacc, blk, stat, tb, dqt, wown, wmine, wpeer, wz,
    lsem, ssem, ctx_sem, sib_sem, blk_sem, stat_sem, tok_sem, dq_sem, wp_sem, wz_sem, out_sem,
):
    e = lax.axis_index("enc")
    d = lax.axis_index("dec")
    y, low = e // 4, e % 4
    core = e % 2
    yup = lax.rem(y + 1, 4) * 4 + low
    ydn = lax.rem(y + 3, 4) * 4 + low
    yfar = lax.rem(y + 2, 4) * 4 + low
    sib = e + 1 - 2 * core
    xflip = e + 2 - 4 * ((e // 2) % 2)
    xh = d // 4

    def peer(m):
        out = d
        for bit in (1, 2, 4):
            if m & bit:
                out = out + bit - 2 * bit * ((d // bit) % 2)
        return out

    dev = {
        "yup": (yup, d), "ydn": (ydn, d), "yfar": (yfar, d), "sib": (sib, d),
        "xi": (xflip, d), "xo": (xflip, peer(4)),
    }
    partner = [(e, peer(m)) for m in range(8)]

    barrier = pltpu.get_barrier_semaphore()
    greet = list(dev.values()) + partner[1:]
    for target in greet:
        pl.semaphore_signal(barrier, inc=1, device_id=target, device_id_type=MESH)

    loads = []

    def load(src, dst):
        copy = pltpu.make_async_copy(src, dst, lsem.at[len(loads)])
        copy.start()
        loads.append(copy)
        return copy

    l_own = [load(r, own.at[i]) for i, r in enumerate((sk_h, sv_h, sq_h, gs_h))]
    l_ctx = [load(ctx_h.at[pl.ds(a * 128, 128)], ctx.at[0, a, 0]) for a in range(2)]
    l_wk = load(wk_h, wkv.at[:, pl.ds(0, ROWS)])
    l_wv = load(wv_h, wkv.at[:, pl.ds(ROWS, ROWS)])
    l_gc = load(gc_h, gc)
    l_tok = load(tok_h, tok)
    l_wq = load(wq_h, wq)

    leaving = []

    def store(src, dst):
        copy = pltpu.make_async_copy(src, dst, out_sem.at[len(leaving)])
        copy.start()
        leaving.append(copy)

    sent = {}

    def send(kind, src, dst, rsem, target):
        group = list(sent).index(kind) if kind in sent else len(sent)
        pltpu.make_async_remote_copy(
            src_ref=src, dst_ref=dst, send_sem=ssem.at[group], recv_sem=rsem,
            device_id=target, device_id_type=MESH,
        ).start()
        sent[kind] = sent.get(kind, 0) + math.prod(src.shape)

    def sent_all(kind, whole):
        assert sent[kind] == math.prod(whole.shape), kind
        pltpu.make_async_remote_copy(
            src_ref=whole, dst_ref=whole, send_sem=ssem.at[list(sent).index(kind)],
            recv_sem=lsem.at[0], device_id=dev["sib"], device_id_type=MESH,
        ).wait_send()

    def arrived(dst, rsem):
        pltpu.make_async_remote_copy(
            src_ref=dst, dst_ref=dst, send_sem=ssem.at[0], recv_sem=rsem,
            device_id=dev["sib"], device_id_type=MESH,
        ).wait_recv()

    quarter = ROWS // 4
    slots = {}

    def slot_sem(k, i):
        alone = k in (2, 6) or (k, i) in ((7, 0), (7, 1), (3, 2), (3, 3))
        return ctx_sem.at[slots.setdefault((k, i if alone else i // 2 * 2), len(slots))]

    def part(k, i, side=0):
        return ctx.at[k, i // 2, side, pl.ds(i % 2 * quarter, quarter), :]

    def pair(k, a, side=0):
        return ctx.at[k, a, side]

    def pass_on(src, k, i, target):
        send("context", src, part(k, i), slot_sem(k, i), target)

    def got(k, i):
        arrived(part(k, i), slot_sem(k, i))

    def got_pair(k, a):
        arrived(pair(k, a), slot_sem(k, 2 * a))
        share_pair(k, a)

    def share(k, i):
        send("share", part(k, i), part(k, i, 1), sib_sem.at[2 * k + i // 2], dev["sib"])

    def share_pair(k, a):
        send("share", pair(k, a), pair(k, a, 1), sib_sem.at[2 * k + a], dev["sib"])

    def shared(k, halves_=(0, 1)):
        for a in halves_:
            arrived(pair(k, a, 1), sib_sem.at[2 * k + a])

    for c in l_own:
        c.wait()
    for c in l_ctx:
        c.wait()
    pl.semaphore_wait(barrier, len(greet))

    def own_block(m):
        bit = (d // (1 if m == 1 else 2 if m < 4 else 4)) % 2
        return own.at[pl.ds(2 * bit, 2)]

    def blk_out(m, slot, src):
        spot = 1 if slot == 4 else 0 if slot < 4 else 2
        send("block", src, blk.at[slot], blk_sem.at[spot], partner[m])

    blk_out(4, 4, own_block(4))
    for i in (0, 1):
        pass_on(part(0, i), 6, i, dev["yup"])
        pass_on(part(0, 2 + i), 2, 2 + i, dev["ydn"])
    for a in range(2):
        share_pair(0, a)
    for i in (0, 1):
        pass_on(part(0, 2 + i), 6, 2 + i, dev["yup"])
        pass_on(part(0, i), 2, i, dev["ydn"])
    for m in (1, 3, 2):
        blk_out(m, m, own_block(m))

    l_wk.wait()
    l_wv.wait()
    wkvt[...] = wkv[...].T
    l_tok.wait()
    l_wq.wait()
    cq = nn(tok[...], wq[...]).astype(BF16)
    cqt = cq.T
    l_gc.wait()
    gcv = gc[...]
    gct = gcv.T

    def hs(h):
        return slice(h * HD, (h + 1) * HD)

    ctx2 = ctx.reshape(16 * ROWS, ctx.shape[4])

    def span(k):
        return slice(k * 2 * ROWS, (k + 1) * 2 * ROWS)

    def lanes(f, x):
        out = x[:, :HD]
        for i in range(1, x.shape[1] // HD):
            out = f(out, x[:, i * HD:(i + 1) * HD])
        return out

    def unit(k, half):
        return slice((2 * k + half) * ROWS, (2 * k + half + 1) * ROWS)

    def cross_scores(k, first=False, half=None):
        cols = span(k) if half is None else unit(k, half)
        x = ctx2[cols]
        kv = [nt(wkvt[i * ROWS:(i + 1) * ROWS], x).astype(BF16) for i in range(2)]
        for i in range(2):
            kvt[i * ROWS:(i + 1) * ROWS, cols] = kv[i]
        for h in range(2):
            s = nn(cq[:, hs(h)], kv[0][hs(h)]) * SCALE
            wst[h, :, cols] = s
            top = lanes(jnp.maximum, s)
            cm[h] = top if first else jnp.maximum(cm[h], top)
            dpst[h, :, cols] = nn(gcv[:, hs(h)], kv[1][hs(h)]) * SCALE

    def cross_weights(g, chunks):
        for h in range(2):
            top = jnp.max(cm[h], axis=1, keepdims=True)
            mst[g, h] = top
            add_l, add_o = None, None
            for cols in chunks:
                w = jnp.exp(wst[h, :, cols] - top)
                wst[h, :, cols] = w
                one_l = lanes(jnp.add, w)
                one_o = nt(w.astype(BF16), kvt[ROWS + h * HD:ROWS + (h + 1) * HD, cols])
                add_l = one_l if add_l is None else add_l + one_l
                add_o = one_o if add_o is None else add_o + one_o
            if g:
                fix = jnp.exp(mst[g - 1, h] - top)
                add_l = add_l + cl[h] * fix
                add_o = add_o + cacc[h] * fix
            cl[h] = add_l
            cacc[h] = add_o

    groups = (
        (span(0), span(6), span(2)),
        (span(1), span(4), unit(7, 0), unit(3, 1)),
        (unit(7, 1), unit(3, 0), span(5)),
    )

    row = lax.broadcasted_iota(jnp.int32, (ROWS, ROWS), 0)
    col = lax.broadcasted_iota(jnp.int32, (ROWS, ROWS), 1)

    def xor_slot(p):
        out = 0
        for bit in (1, 2, 4):
            out = out + bit * (((d // bit) + (p // bit)) % 2)
        return out

    def halves(f, x):
        return f(x[:, :HD], x[:, HD:])

    def self_scores(p, carry):
        slot = xor_slot(p)
        for h in range(2):
            s = nt(own[2, :, hs(h)], blk[slot, 0, :, hs(h)]) * SCALE
            sst[slot, h] = s
            sm[h] = jnp.maximum(sm[h], halves(jnp.maximum, s))
        return carry

    def self_weights(p, carry):
        slot = xor_slot(p)
        for h in range(2):
            w = jnp.exp(sst[slot, h] - st_top[h])
            sl[h] += halves(jnp.add, w)
            sacc[h] += nn(w.astype(BF16), blk[slot, 1, :, hs(h)])
        return carry

    shared(0)
    cross_scores(0, True)
    got_up = lambda i: (
        got(6, i),
        pass_on(part(6, i), 4, i, dev["yup"]) if i < 2 else None,
        pass_on(part(6, i), 7, i, dev["xi"] if i < 2 else dev["xo"]),
        share(6, i),
    )
    got_down = lambda i: (
        got(2, i),
        pass_on(part(2, i), 4, i, dev["ydn"]) if i > 1 else None,
        pass_on(part(2, i), 3, i, dev["xi"] if i < 2 else dev["xo"]),
        share(2, i),
    )
    got_up(0)
    got_down(2)
    for h in range(2):
        s = jnp.where(row >= col, nt(own[2, :, hs(h)], own[0, :, hs(h)]) * SCALE, -1e30)
        sst[0, h] = s
        sm[h] = halves(jnp.maximum, s)
    got_up(1)
    got_down(3)
    for i in range(2):
        send("context", pair(0, i), pair(1, i), slot_sem(1, 2 * i), dev["xo" if i else "xi"])
    arrived(blk.at[4], blk_sem.at[1])
    for m in (1, 3, 2):
        blk_out(m, 4 + m, blk.at[4])
    shared(6, (0,))
    cross_scores(6, half=0)
    got_up(2)
    got_down(0)
    shared(2, (1,))
    cross_scores(2, half=1)
    got_up(3)
    got_down(1)
    shared(6, (1,))
    cross_scores(6, half=1)
    shared(2, (0,))
    cross_scores(2, half=0)
    for i in (0, 1):
        got(7, i)
        pass_on(part(7, i), 5, i, dev["yup"])
        share(7, i)
        got(3, 2 + i)
        pass_on(part(3, 2 + i), 5, 2 + i, dev["ydn"])
        share(3, 2 + i)
    arrived(blk.at[pl.ds(1, 3)], blk_sem.at[0])
    lax.fori_loop(4 * xh, d, self_scores, 0)
    shared(7, (0,))
    cross_scores(7, half=0)
    shared(3, (1,))
    cross_scores(3, half=1)
    cross_weights(0, groups[0])
    for a in range(2):
        got_pair(1, a)
    for a in range(2):
        got_pair(4, a)
    for h in range(2):
        top = jnp.max(sm[h], axis=1, keepdims=True)
        st_top[h] = top
        w = jnp.exp(sst[0, h] - top)
        sl[h] = halves(jnp.add, w)
        sacc[h] = nn(w.astype(BF16), own[1, :, hs(h)])
    lax.fori_loop(4 * xh, d, self_weights, 0)
    shared(1)
    cross_scores(1)
    shared(4)
    cross_scores(4)
    cross_weights(1, groups[1])
    got_pair(7, 1)
    got_pair(3, 0)
    for a in range(2):
        got_pair(5, a)
    shared(7, (1,))
    cross_scores(7, half=1)
    shared(3, (0,))
    cross_scores(3, half=0)
    lane = (y * 2 + core) * 32
    trows = pl.ds(pl.multiple_of(lane, 32), 32)

    def tcols(p):
        return pl.ds(pl.multiple_of(p * 512, 512), 512)

    for m in range(1, 8):
        send("columns", tok.at[trows, tcols(partner[m][1])], tb.at[m, trows], tok_sem.at[0], partner[m])
    l_tb = load(tok.at[:, tcols(d)], tb.at[0])
    shared(5)
    cross_scores(5)
    cross_weights(2, groups[2])

    def weight_part(h, group):
        return nn(dkvt[h], ctx2[:, pl.ds(pl.multiple_of(group * 512, 512), 512)])

    def dq_slot(m, h):
        return dqt.at[m, pl.ds(h * HD, HD), :]

    def trange(ee):
        return pl.ds(pl.multiple_of((ee // 4 * 2 + ee % 2) * 32, 32), 32)

    def gather_tokens():
        moved = tb.at[pl.ds(1, 7), trows]
        arrived(moved, tok_sem.at[0])
        l_tb.wait()
        for name in ("yup", "ydn", "yfar", "sib"):
            send("rows", moved, moved, tok_sem.at[1], dev[name])

    def send_pieces(h, pieces):
        for m in pieces:
            spot = partner[m][1] - 4 * xh
            send("peer", wmine.at[h, spot], wpeer.at[h, spot], wp_sem.at[h, m], partner[4])

    def peer_weights(h):
        piece = weight_part(h, 1 - xh).astype(BF16)
        for z in range(4):
            wmine[h, z] = piece[:, z * HD:(z + 1) * HD]
        send_pieces(h, (2, 1, 3))

    for h in range(2):
        norm = jnp.sum(cl[h], axis=1, keepdims=True)
        out = (cacc[h] / norm).astype(BF16)
        o_cross[:, hs(h)] = out
        g = gcv[:, hs(h)]
        lse = mst[2, h] + jnp.log(norm)
        delta = jnp.sum(g.astype(F32) * out.astype(F32), axis=1, keepdims=True) * SCALE
        for i, chunks in enumerate(groups):
            fix = jnp.exp(mst[i, h] - lse)
            for cols in chunks:
                p = wst[h, :, cols] * fix
                prob[:, cols] = p.astype(BF16)
                dscore[:, cols] = (p * (dpst[h, :, cols] - delta)).astype(BF16)
        dq = nt(dscore[...], kvt[hs(h), :])
        dqt[0, hs(h), :] = dq.astype(BF16).T
        for m in (4, 1, 3, 2):
            send("dq", dq_slot(0, h), dq_slot(m, h), dq_sem.at[h if m == 4 else 2], partner[m])
        dkvt[h, 0:HD, :] = nn(cqt[hs(h)], dscore[...]).astype(BF16)
        dkvt[h, HD:, :] = nn(gct[hs(h)], prob[...]).astype(BF16)
        if h == 0:
            peer_weights(0)
            gather_tokens()

    def forward_dq(h):
        arrived(dq_slot(4, h), dq_sem.at[h])
        for m in (1, 3, 2):
            send("dq", dq_slot(4, h), dq_slot(4 + m, h), dq_sem.at[3], partner[m])

    def sum_and_pass(h):
        for m in (2, 1, 3):
            spot = partner[m][1] - 4 * xh
            arrived(wpeer.at[h, spot], wp_sem.at[h, m])
            wpeer[h, spot] = (wown[h, spot] + wpeer[h, spot].astype(F32)).astype(BF16)
            send("sum", wpeer.at[h, spot], wz.at[m, h], wz_sem.at[0], partner[m])

    def own_weights(h):
        piece = weight_part(h, xh)
        for z in range(4):
            wown[h, z] = piece[:, z * HD:(z + 1) * HD]

    peer_weights(1)
    forward_dq(0)
    own_weights(0)
    arrived(blk.at[pl.ds(5, 3)], blk_sem.at[2])
    lax.fori_loop(0, 4 * xh, self_scores, 0)
    for h in range(2):
        top = jnp.max(sm[h], axis=1, keepdims=True)
        fix = jnp.exp(st_top[h] - top)
        st_top[h] = top
        sl[h] = sl[h] * fix
        sacc[h] = sacc[h] * fix
    lax.fori_loop(0, 4 * xh, self_weights, 0)
    for h in range(2):
        norm = jnp.sum(sl[h], axis=1, keepdims=True)
        out = (sacc[h] / norm).astype(BF16)
        o_self[:, hs(h)] = out
        g = own[3, :, hs(h)]
        lse = st_top[h] + jnp.log(norm)
        delta = jnp.sum(g.astype(F32) * out.astype(F32), axis=1, keepdims=True)
        sm[h] = jnp.broadcast_to(lse, (ROWS, HD))
        sl[h] = jnp.broadcast_to(delta, (ROWS, HD))
        stat[0, 2 * h:2 * h + 1, :] = sm[h].T[0:1]
        stat[0, 2 * h + 1:2 * h + 2, :] = sl[h].T[0:1]
    store(o_self, r_self)
    store(o_cross, r_cross)
    for m in range(1, 8):
        send("stat", stat.at[0], stat.at[m], stat_sem.at[0], partner[m])
    for h in range(2):
        send_pieces(h, (0,))
    sum_and_pass(0)
    own_weights(1)
    forward_dq(1)
    def query_grad(h, s, v, k):
        p = jnp.exp(s - sm[h, :, 0:1])
        dp = nt(own[3, :, hs(h)], v)
        return nn((p * (dp - sl[h, :, 0:1]) * SCALE).astype(BF16), k)

    for h in range(2):
        o_dsq[:, hs(h)] = query_grad(h, sst[0, h], own[1, :, hs(h)], own[0, :, hs(h)])

    def self_query(p, carry):
        slot = xor_slot(p)
        for h in range(2):
            o_dsq[:, hs(h)] += query_grad(
                h, sst[slot, h], blk[slot, 1, :, hs(h)], blk[slot, 0, :, hs(h)]
            )
        return carry

    lax.fori_loop(0, d, self_query, 0)
    store(o_dsq, r_dsq)

    sum_and_pass(1)
    arrived(tb.at[pl.ds(1, 7), pl.ds(0, 128)], tok_sem.at[1])
    for ee in (ydn, yup, yfar):
        spot = tb.at[pl.ds(1, 7), trange(ee)]
        send("rows", spot, spot, tok_sem.at[2], dev["sib"])

    def key_grad(h, st, q, g, lse, delta):
        p = jnp.exp(st - lse)
        dp = nt(own[1, :, hs(h)], g)
        ds = (p * (dp - delta) * SCALE).astype(BF16)
        return nn(ds, q), nn(p.astype(BF16), g)

    for h in range(2):
        q, g = own[2, :, hs(h)], own[3, :, hs(h)]
        st = jnp.where(col >= row, nt(own[0, :, hs(h)], q) * SCALE, -1e30)
        dk, dv = key_grad(h, st, q, g, stat[0, 2 * h:2 * h + 1], stat[0, 2 * h + 1:2 * h + 2])
        o_dsk[:, hs(h)] = dk
        o_dsv[:, hs(h)] = dv
    arrived(stat.at[pl.ds(1, 7)], stat_sem.at[0])

    def self_key(p, carry):
        slot = xor_slot(p)
        for h in range(2):
            q, g = blk[slot, 0, :, hs(h)], blk[slot, 1, :, hs(h)]
            st = nt(own[0, :, hs(h)], q) * SCALE
            dk, dv = key_grad(
                h, st, q, g, stat[slot, 2 * h:2 * h + 1], stat[slot, 2 * h + 1:2 * h + 2]
            )
            o_dsk[:, hs(h)] += dk
            o_dsv[:, hs(h)] += dv
        return carry

    lax.fori_loop(d + 1, 8, self_key, 0)
    store(o_dsk, r_dsk)
    store(o_dsv, r_dsv)
    arrived(tb.at[pl.ds(1, 7), pl.ds(0, 96)], tok_sem.at[2])
    arrived(dqt.at[pl.ds(1, 3)], dq_sem.at[2])
    arrived(dqt.at[pl.ds(5, 3)], dq_sem.at[3])
    gw = None
    for m in range(8):
        add = nn(dqt[m], tb[m])
        gw = add if gw is None else gw + add
    o_gwq[...] = gw.T
    store(o_gwq, r_gwq)
    arrived(wz.at[pl.ds(1, 3)], wz_sem.at[0])
    mine = d - 4 * xh
    for h in range(2):
        arrived(wpeer.at[h, mine], wp_sem.at[h, 0])
        total = wown[h, mine] + wpeer[h, mine].astype(F32)
        for m in (1, 2, 3):
            total = total + wz[m, h].astype(F32)
        o_gwk[:, hs(h)] = total[0:HD].T
        o_gwv[:, hs(h)] = total[HD:].T
    store(o_gwk, r_gwk)
    store(o_gwv, r_gwv)

    sent_all("context", ctx.at[pl.ds(0, 7), :, 0])
    sent_all("share", ctx.at[:, :, 0])
    sent_all("block", blk.at[pl.ds(0, 7)])
    sent_all("columns", tb.at[pl.ds(1, 7), pl.ds(0, 32)])
    sent_all("rows", tb.at[pl.ds(1, 7), pl.ds(0, 224)])
    sent_all("peer", wmine)
    sent_all("dq", dqt.at[pl.ds(0, 7)])
    sent_all("sum", wz.at[pl.ds(1, 3)])
    sent_all("stat", stat.at[pl.ds(1, 7)])
    for copy in leaving:
        copy.wait()


def hand_over(*refs):
    sources, targets, held, sem = refs[:8], refs[8:16], refs[16:24], refs[24]
    loads = [
        pltpu.make_async_copy(a, b, sem.at[0, i]) for i, (a, b) in enumerate(zip(sources, held))
    ]
    stores = [
        pltpu.make_async_copy(a, b, sem.at[1, i]) for i, (a, b) in enumerate(zip(held, targets))
    ]
    for copy in loads:
        copy.start()
    for copy, store in zip(loads, stores):
        copy.wait()
        store.start()
    for store in stores:
        store.wait()


def body(*args):
    any_ = pl.BlockSpec(memory_space=pl.ANY)
    shape = jax.ShapeDtypeStruct
    block = (ROWS, ROWS)
    dma = pltpu.SemaphoreType.DMA
    shapes = (
        shape(block, BF16), shape(block, F32), shape(block, F32), shape(block, F32),
        shape(block, BF16), shape((512, ROWS), F32), shape((128, ROWS), F32),
        shape((128, ROWS), F32),
    )
    results = pl.pallas_call(
        kernel,
        out_shape=shapes,
        in_specs=[any_] * 10,
        out_specs=[any_] * 8,
        scratch_shapes=[pltpu.VMEM(x.shape, x.dtype) for x in shapes] + [
            pltpu.VMEM((256, 4096), BF16),
            pltpu.VMEM((4096, 256), BF16),
            pltpu.VMEM((1024, 512), BF16),
            pltpu.VMEM((512, 1024), BF16),
            pltpu.VMEM((4, 256, 256), BF16),
            pltpu.VMEM((256, 256), BF16),
            pltpu.VMEM((8, 2, 2, 128, 1024), BF16),
            pltpu.VMEM((512, 4096), BF16),
            pltpu.VMEM((2, 256, 4096), F32),
            pltpu.VMEM((2, 256, 4096), F32),
            pltpu.VMEM((4, 2, 256, 1), F32),
            pltpu.VMEM((2, 256, 4096), BF16),
            pltpu.VMEM((256, 4096), BF16),
            pltpu.VMEM((256, 4096), BF16),
            pltpu.VMEM((2, 256, 128), F32),
            pltpu.VMEM((2, 256, 128), F32),
            pltpu.VMEM((2, 256, 128), F32),
            pltpu.VMEM((2, 256, 1), F32),
            pltpu.VMEM((8, 2, 256, 256), F32),
            pltpu.VMEM((2, 256, 128), F32),
            pltpu.VMEM((2, 256, 128), F32),
            pltpu.VMEM((2, 256, 128), F32),
            pltpu.VMEM((8, 2, 256, 256), BF16),
            pltpu.VMEM((8, 8, 256), F32),
            pltpu.VMEM((8, 256, 512), BF16),
            pltpu.VMEM((8, 256, 256), BF16),
            pltpu.VMEM((2, 4, 256, 128), F32),
            pltpu.VMEM((2, 4, 256, 128), BF16),
            pltpu.VMEM((2, 4, 256, 128), BF16),
            pltpu.VMEM((4, 2, 256, 128), BF16),
            dma((12,)), dma((9,)), dma((20,)), dma((16,)), dma((3,)), dma((1,)), dma((3,)),
            dma((4,)), dma((2, 4)), dma((1,)), dma((8,)),
        ],
        compiler_params=pltpu.CompilerParams(
            collective_id=0, has_side_effects=True, vmem_limit_bytes=62 << 20
        ),
        name="layer",
    )(*args)
    return tuple(pl.pallas_call(
        hand_over,
        out_shape=shapes,
        in_specs=[any_] * 8,
        out_specs=[any_] * 8,
        scratch_shapes=[pltpu.VMEM(x.shape, x.dtype) for x in shapes] + [dma((2, 8))],
        name="hand_over",
    )(*results))


def solution(mesh):
    placed = (
        P("dec", None), P(None, "enc"), P("enc", None), P(None, "enc"), P(None, "enc"),
    ) + (P("dec", "enc"),) * 5
    return jax.shard_map(
        body, mesh=mesh, in_specs=placed, out_specs=(P("dec", "enc"),) * 8, check_vma=False
    )
```
